32 devices in a mesh: dp: 4 (over x, core), vocab: 4 (over z), tensor: 2 (over y).
Axes of the slice: x: 2, y: 2, z: 4, core: 2. Of those that a mesh axis runs over, the one named last changes fastest.
Arguments:
- residual: bfloat16 [352, 4096], P('dp', 'tensor'), may hold values from -400 to 400
- norm_gain: float32 [4096], P('tensor'), may hold values from 0.1 to 1.9
- gain_dir: float32 [4096], P('tensor'), may hold values from -6 to 6
- head_weight: bfloat16 [4096, 10240], P('tensor', ('dp', 'vocab')), may hold values from -0.8 to 0.8
- head_dir: bfloat16 [4096, 10240], P('tensor', ('dp', 'vocab')), may hold values from -0.25 to 0.25
- sampled: int32 [352], replicated, may hold values from 0 to 10239
Outputs:
- fisher_head: float32 [4096, 10240], P('tensor', ('dp', 'vocab'))
- fisher_gain: float32 [4096], P('tensor')
The draws below stay inside these ranges and needn't reach their ends.
All inputs are finite; a program needn't handle non-finite values.
Results may differ from the reference program's by a relative error of at most 0.012.
The reference program's roundings to bfloat16 on the way (of `normed`, `hidden`, `tangent` and `cotangent`) count: a program that leaves them out, or rounds other values in their place, can miss the bound.
Values may be sent and summed in bfloat16 or wider, within the bound.
A program may use at most 128 MiB of HBM per device.

```python
import math
import jax
import jax.numpy as jnp
import numpy as np
from jax import lax

D = 4096
TOKENS = 352
VOCAB = 10240


def draw_residual(key, part):
    key = jax.random.fold_in(key, 3)
    noise_key, row_key, col_key = jax.random.split(key, 3)
    row_scale = jnp.exp(jax.random.uniform(row_key, (TOKENS, 1), jnp.float32) * math.log(10.0))
    col_scale = jnp.exp(jax.random.uniform(col_key, (1, D), jnp.float32) * math.log(10.0))
    noise = jnp.clip(jax.random.normal(noise_key, (TOKENS, D), jnp.float32), -4.0, 4.0)
    entries = noise * row_scale * col_scale
    return entries.astype(jnp.bfloat16)


def draw_head_weight(key, part):
    key = jax.random.fold_in(key, 5)
    noise_key, col_key = jax.random.split(key)
    ramp = 1.0 + 2.0 * jnp.arange(VOCAB).astype(jnp.float32) / VOCAB
    col_scale = jnp.exp(jax.random.uniform(col_key, (1, VOCAB), jnp.float32) * math.log(10.0)) * 0.4 * ramp[None, :] / math.sqrt(D)
    noise = jnp.clip(jax.random.normal(noise_key, (D, VOCAB), jnp.float32), -4.0, 4.0)
    entries = noise * col_scale
    return entries.astype(jnp.bfloat16)


def plant(values, key, least, top_value):
    longest = values.shape.index(max(values.shape))
    spots = []
    for shift in (0, 1):
        where = [jax.random.randint(jax.random.fold_in(key, axis), (), 0, length) for axis, length in enumerate(values.shape)]
        where[longest] = (where[longest] + shift) % values.shape[longest]
        spots.append(tuple(where))
    return values.at[spots[0]].set(least).at[spots[1]].set(top_value)


def level_of(key, extent, pieces, low, high):
    gain = 1.0
    for position, shards_of in pieces:
        draws = jax.random.uniform(jax.random.fold_in(jax.random.fold_in(key, 6), position), (shards_of,), jnp.float32, low / len(pieces), high / len(pieces))
        gain = gain * jnp.repeat(jnp.exp(draws), extent[position] // shards_of).reshape((-1,) + (1,) * (len(extent) - 1 - position))
    return gain


def rank_bounds(amount, lean):
    loads = [(1 << 20) // math.isqrt(grade ** lean) + 1 for grade in range(1, amount + 1)]
    scale = 1 + sum(loads) // (1 << 30)
    return np.cumsum(np.array([max(1, weight // scale) for weight in loads]))


def ranked_ids(own_key, shape, count, slope):
    listing = rank_bounds(count, slope)
    lot = jax.random.randint(jax.random.fold_in(own_key, 1), shape, 0, int(listing[count - 1]))
    standing = jnp.searchsorted(jnp.asarray(listing, jnp.int32), lot, side="right")
    return jax.random.permutation(jax.random.fold_in(own_key, 2), count)[standing].astype(jnp.int32)


def centred(stream_key, shape, scale, most, shards=(), kind=jnp.bfloat16):
    values = scale * jax.random.normal(stream_key, shape, jnp.float32)
    if shards:
        values = values * level_of(stream_key, shape, shards, -0.22, 0.18)
    return jnp.clip(values, -most, most).astype(kind)


def setup_inputs(seed: int = 0) -> dict:
    keys = jax.random.split(jax.random.key(seed), 7)
    residual = draw_residual(jax.random.fold_in(keys[6], 71), 0)
    norm_gain = jnp.clip(1.0 + 0.18 * jax.random.normal(keys[1], (D,), jnp.float32), 0.1, 1.9)
    gain_dir = centred(keys[2], (D,), 1.0, 6.0, ((0, 2),), jnp.float32)
    head_weight = draw_head_weight(jax.random.fold_in(keys[6], 71), 0)
    head_dir = centred(keys[4], (D, VOCAB), (D // 9) ** -0.5, 0.25, ((0, 2), (1, 16)))
    sampled = plant(ranked_ids(keys[5], (TOKENS,), VOCAB, 2), jax.random.fold_in(keys[5], 3), 0, VOCAB - 1).astype(jnp.int32)
    return dict(residual=residual, norm_gain=norm_gain, gain_dir=gain_dir, head_weight=head_weight, head_dir=head_dir, sampled=sampled)


EPSILON = 1e-06

def reference(residual, norm_gain, gain_dir, head_weight, head_dir, sampled):
    entries = residual.astype(jnp.float32)
    inverse = lax.rsqrt(lax.optimization_barrier(jnp.mean(entries * entries, axis=1, keepdims=True)) + EPSILON)
    normed = (entries * inverse).astype(jnp.bfloat16)
    spread = normed.astype(jnp.float32)
    hidden = (spread * norm_gain).astype(jnp.bfloat16)
    tangent = (spread * gain_dir).astype(jnp.bfloat16)
    logits = jnp.dot(hidden, head_weight, preferred_element_type=jnp.float32)
    tangent_logits = jnp.dot(hidden, head_dir, preferred_element_type=jnp.float32) + jnp.dot(tangent, head_weight, preferred_element_type=jnp.float32)
    row_top = lax.optimization_barrier(jnp.max(logits, axis=1, keepdims=True))
    scaled_exp = jnp.exp(logits - row_top)
    row_total = lax.optimization_barrier(jnp.sum(scaled_exp, axis=1, keepdims=True))
    row_probs = scaled_exp / row_total
    weighted = lax.optimization_barrier(jnp.sum(scaled_exp * tangent_logits, axis=1, keepdims=True)) / row_total
    picked = jnp.take_along_axis(tangent_logits, sampled[:, None].astype(jnp.int32), axis=1)
    is_picked = (jnp.arange(logits.shape[1], dtype=jnp.int32)[None, :] == sampled[:, None].astype(jnp.int32)).astype(jnp.float32)
    cotangent = ((picked - weighted) * (is_picked - row_probs)).astype(jnp.bfloat16)
    product = lax.dot_general(normed, cotangent, (((0,), (0,)), ((), ())), preferred_element_type=jnp.float32)
    fisher_head = norm_gain[:, None] * product
    fisher_gain = lax.optimization_barrier(jnp.sum(head_weight.astype(jnp.float32) * product, axis=1))
    return (fisher_head, fisher_gain)
```

```python
import functools

import jax
import jax.numpy as jnp
from jax import lax
from jax.experimental import pallas as pl
from jax.experimental.pallas import tpu as pltpu
from jax.sharding import PartitionSpec as P

EPSILON = 1e-06
LANES = 128
CHUNKS = 4
MIB = 1024 * 1024


def remote(src, dst, send_sem, recv_sem, device):
    return pltpu.make_async_remote_copy(
        src_ref=src,
        dst_ref=dst,
        send_sem=send_sem,
        recv_sem=recv_sem,
        device_id=device,
        device_id_type=pl.DeviceIdType.MESH,
    )


def merge(parts):
    top = functools.reduce(jnp.maximum, [part[0] for part in parts])
    scales = [jnp.exp(part[0] - top) for part in parts]
    total = sum(part[1] * scale for part, scale in zip(parts, scales))
    weighted = sum(part[2] * scale for part, scale in zip(parts, scales))
    picked = sum(part[3] for part in parts)
    return top, total, weighted, picked


def kernel(
    n_dp, n_v, res_ref, gain_ref, dir_ref, ids_ref, w_hbm, h_hbm, n_out, c_out, g_out,
    x, w, h, normed, hid, tan, lg, tl, tb, rl, rt, eb, co, ss, sl, sz, sp, gz, gp,
    in_sem, out_sem, ss_s, ss_r, xs_s, xs_r, cs_s, cs_r, ls_s, ls_r, ts_s, ts_r, es_s, es_r,
    sl_s, sl_r, sz_s, sz_r, sp_s, sp_r, gz_s, gz_r, gp_s, gp_r,
):
    n_hi = n_dp // 2
    rows, depth = res_ref.shape
    vocab = w.shape[1]
    pad = x.shape[2]
    width = x.shape[3]
    f32, bf16 = jnp.float32, jnp.bfloat16
    me, v, t = lax.axis_index("dp"), lax.axis_index("vocab"), lax.axis_index("tensor")
    core, my_hi = me % 2, me // 2
    other = 1 - t
    place = me * 2 + t
    mate = me + 1 - 2 * core
    core_peer, y_peer = {"dp": mate}, {"tensor": other}
    plane = [(place + k) % (2 * n_dp) for k in range(1, 2 * n_dp)]
    column = [(v + k) % n_v for k in range(1, n_v)]
    ring = [(me + k) % n_dp for k in range(1, n_dp)]

    load_w = pltpu.make_async_copy(w_hbm, w, in_sem.at[0])
    load_h = pltpu.make_async_copy(h_hbm, h, in_sem.at[1])
    load_w.start()
    load_h.start()

    barrier = pltpu.get_barrier_semaphore()
    for p in plane:
        pl.semaphore_signal(
            barrier, inc=1, device_id={"dp": p // 2, "tensor": p % 2},
            device_id_type=pl.DeviceIdType.MESH,
        )
    for z in column:
        pl.semaphore_signal(
            barrier, inc=1, device_id={"vocab": z}, device_id_type=pl.DeviceIdType.MESH
        )

    mask = lax.broadcasted_iota(jnp.int32, (pad, LANES), 0) == lax.broadcasted_iota(
        jnp.int32, (pad, LANES), 1
    )

    def to_row(col):
        return jnp.sum(jnp.where(mask, col, 0.0), axis=0, keepdims=True)

    def to_col(row):
        return jnp.sum(jnp.where(mask, row, 0.0), axis=1, keepdims=True)

    squares = jnp.zeros((pad, 1), f32)
    for c in range(CHUNKS):
        part = res_ref[:, c * width:(c + 1) * width].astype(f32)
        part = jnp.concatenate([part, jnp.zeros((pad - rows, width), f32)], axis=0)
        squares = squares + jnp.sum(part * part, axis=1, keepdims=True)
        x[me, c] = part.astype(bf16)
    ss[me, t] = to_row(squares)

    pl.semaphore_wait(barrier, len(plane) + len(column))

    for p in plane:
        remote(
            ss.at[me, t], ss.at[me, t], ss_s.at[p // 2, p % 2], ss_r.at[me, t],
            {"dp": p // 2, "tensor": p % 2},
        ).start()
    for c in range(CHUNKS):
        remote(x.at[me, c], x.at[me, c], cs_s.at[my_hi, c], cs_r.at[my_hi, c], core_peer).start()
    for c in range(CHUNKS):
        for k in range(1, n_hi):
            hi = (my_hi + k) % n_hi
            remote(
                x.at[me, c], x.at[me, c], xs_s.at[hi, c], xs_r.at[my_hi, c], {"dp": hi * 2 + core}
            ).start()

    def wait_core(hi):
        for c in range(CHUNKS):
            slot = x.at[hi * 2 + 1 - core, c]
            remote(slot, slot, cs_s.at[hi, c], cs_r.at[hi, c], core_peer).wait_recv()

    for p in plane:
        slot = ss.at[p // 2, p % 2]
        remote(
            slot, slot, ss_s.at[p // 2, p % 2], ss_r.at[p // 2, p % 2],
            {"dp": p // 2, "tensor": p % 2},
        ).wait_recv()

    def out_copy(hi):
        return pltpu.make_async_copy(normed.at[hi], n_out.at[hi], out_sem.at[0, hi])

    def send_logits(hi):
        return remote(
            lg.at[hi, other, pl.ds(0, rows)], rl.at[hi], ls_s.at[hi], ls_r.at[hi], y_peer
        )

    def send_tangents(hi):
        return remote(tb.at[hi], rt.at[hi], ts_s.at[hi], ts_r.at[hi], y_peer)

    def pair(hi, first):
        inverse = jnp.concatenate(
            [
                to_col(lax.rsqrt((ss[hi * 2 + k, 0] + ss[hi * 2 + k, 1]) / (2 * depth) + EPSILON))
                for k in range(2)
            ],
            axis=0,
        )
        for c in range(CHUNKS):
            at = slice(c * width, (c + 1) * width)
            block = jnp.concatenate(
                [x[hi * 2, c].astype(f32), x[hi * 2 + 1, c].astype(f32)], axis=0
            )
            unit = (block * inverse).astype(bf16)
            normed[hi, :, at] = unit
            spread = unit.astype(f32)
            hid[:, at] = (spread * gain_ref[:, at]).astype(bf16)
            tan[:, at] = (spread * dir_ref[:, at]).astype(bf16)
        out_copy(hi).start()
        if first:
            load_w.wait()
        logits = jnp.dot(hid[...], w[...], preferred_element_type=f32)
        lg[hi, 0] = logits[:pad]
        lg[hi, 1] = logits[pad:]
        send_logits(hi).start()
        if first:
            load_h.wait()
        tangents = jnp.dot(hid[...], h[...], preferred_element_type=f32) + jnp.dot(
            tan[...], w[...], preferred_element_type=f32
        )
        tl[hi, 0] = tangents[:pad]
        tl[hi, 1] = tangents[pad:]
        tb[hi] = tl[hi, other].astype(bf16)
        send_tangents(hi).start()

    wait_core(my_hi)
    pair(my_hi, True)

    def later(k, carry):
        hi = (my_hi + k) % n_hi
        for c in range(CHUNKS):
            slot = x.at[hi * 2 + core, c]
            remote(slot, slot, xs_s.at[hi, c], xs_r.at[hi, c], {"dp": hi * 2 + core}).wait_recv()
            remote(slot, slot, cs_s.at[hi, c], cs_r.at[hi, c], core_peer).start()
        wait_core(hi)
        pair(hi, False)
        return carry

    lax.fori_loop(1, n_hi, later, 0)

    offset = (me * n_v + v) * vocab
    tokens = ids_ref.shape[1]

    def onehot(block):
        here = lax.broadcasted_iota(jnp.int32, (pad, tokens), 0)
        wanted = lax.broadcasted_iota(jnp.int32, (pad, tokens), 1) == here + block * rows
        ids = jnp.sum(
            jnp.where(wanted & (here < rows), ids_ref[...].astype(f32) + 1.0, 0.0),
            axis=1, keepdims=True,
        ).astype(jnp.int32) - 1
        return lax.broadcasted_iota(jnp.int32, (pad, vocab), 1) == ids - offset

    def send_exp(hi):
        return remote(eb.at[hi, t], eb.at[hi, t], es_s.at[hi], es_r.at[hi], y_peer)

    def finish(k, carry):
        hi = (my_hi + k) % n_hi
        send_logits(hi).wait_recv()
        blank = jnp.zeros((pad - rows, vocab), f32)
        logits = jnp.concatenate([lg[hi, t][:rows] + rl[hi], blank], axis=0)
        send_tangents(hi).wait_recv()
        tangents = tl[hi, t] + rt[hi].astype(f32)
        top = jnp.max(logits, axis=1, keepdims=True)
        scaled = jnp.exp(logits - top)
        eb[hi, t] = scaled.astype(bf16)
        chosen = onehot(hi * 2 + t)
        sl[t, hi, 0:1] = to_row(top)
        sl[t, hi, 1:2] = to_row(jnp.sum(scaled, axis=1, keepdims=True))
        sl[t, hi, 2:3] = to_row(jnp.sum(scaled * tangents, axis=1, keepdims=True))
        sl[t, hi, 3:4] = to_row(jnp.sum(jnp.where(chosen, tangents, 0.0), axis=1, keepdims=True))
        return carry

    lax.fori_loop(0, n_hi, finish, 0)

    sz[v] = sl[t]
    for z in column:
        remote(sz.at[v], sz.at[v], sz_s.at[z], sz_r.at[v], {"vocab": z}).start()
    send_local = remote(sl.at[t], sl.at[t], sl_s.at[0], sl_r.at[0], y_peer)
    send_local.start()
    for hi in range(n_hi):
        send_exp(hi).start()
    for z in column:
        remote(sz.at[z], sz.at[z], sz_s.at[z], sz_r.at[z], {"vocab": z}).wait_recv()
    for hi in range(n_hi):
        joined = merge([[sz[z, hi, i:i + 1] for i in range(4)] for z in range(n_v)])
        for i in range(4):
            sp[me, t, hi, i:i + 1] = joined[i]
    for p in plane:
        remote(
            sp.at[me, t], sp.at[me, t], sp_s.at[p // 2, p % 2], sp_r.at[me, t],
            {"dp": p // 2, "tensor": p % 2},
        ).start()
    for p in plane:
        slot = sp.at[p // 2, p % 2]
        remote(
            slot, slot, sp_s.at[p // 2, p % 2], sp_r.at[p // 2, p % 2],
            {"dp": p // 2, "tensor": p % 2},
        ).wait_recv()
    slot = sl.at[other]
    remote(slot, slot, sl_s.at[0], sl_r.at[0], y_peer).wait_recv()

    def cot_copy(hi):
        return pltpu.make_async_copy(co.at[hi], c_out.at[hi], out_sem.at[1, hi])

    def cotangents(hi, grad):
        slot = eb.at[hi, other]
        remote(slot, slot, es_s.at[hi], es_r.at[hi], y_peer).wait_recv()
        both = []
        for k in range(2):
            top, total, weighted, picked = merge(
                [[sp[d, k, hi, i:i + 1] for i in range(4)] for d in range(n_dp)]
            )
            score = to_col(picked - weighted / total)
            factor = to_col(jnp.exp(sl[k, hi, 0:1] - top) / total)
            probs = eb[hi, k].astype(f32) * factor
            both.append(score * (onehot(hi * 2 + k).astype(f32) - probs))
        co[hi] = jnp.concatenate(both, axis=0).astype(bf16)
        cot_copy(hi).start()
        back = lax.dot_general(
            co[hi], w[...], (((1,), (1,)), ((), ())), preferred_element_type=f32
        )
        return grad + jnp.sum(back * normed[hi].astype(f32), axis=0, keepdims=True)

    gz[v] = lax.fori_loop(0, n_hi, cotangents, jnp.zeros((1, depth), f32))
    for z in column:
        remote(gz.at[v], gz.at[v], gz_s.at[z], gz_r.at[v], {"vocab": z}).start()
    for z in column:
        remote(gz.at[z], gz.at[z], gz_s.at[z], gz_r.at[z], {"vocab": z}).wait_recv()
    gp[me] = sum(gz[z] for z in range(n_v))
    for d in ring:
        remote(gp.at[me], gp.at[me], gp_s.at[d], gp_r.at[me], {"dp": d}).start()
    for d in ring:
        remote(gp.at[d], gp.at[d], gp_s.at[d], gp_r.at[d], {"dp": d}).wait_recv()
    g_out[...] = sum(gp[d] for d in range(n_dp))

    for p in plane:
        device = {"dp": p // 2, "tensor": p % 2}
        mine = ss.at[me, t]
        remote(mine, mine, ss_s.at[p // 2, p % 2], ss_r.at[me, t], device).wait_send()
        mine = sp.at[me, t]
        remote(mine, mine, sp_s.at[p // 2, p % 2], sp_r.at[me, t], device).wait_send()
    for z in column:
        remote(sz.at[v], sz.at[v], sz_s.at[z], sz_r.at[v], {"vocab": z}).wait_send()
        remote(gz.at[v], gz.at[v], gz_s.at[z], gz_r.at[v], {"vocab": z}).wait_send()
    for d in ring:
        remote(gp.at[me], gp.at[me], gp_s.at[d], gp_r.at[me], {"dp": d}).wait_send()
    send_local.wait_send()
    for k in range(n_hi):
        hi = (my_hi + k) % n_hi
        for c in range(CHUNKS):
            mine = x.at[hi * 2 + core, c]
            remote(mine, mine, cs_s.at[hi, c], cs_r.at[hi, c], core_peer).wait_send()
            if k:
                mine = x.at[me, c]
                remote(
                    mine, mine, xs_s.at[hi, c], xs_r.at[my_hi, c], {"dp": hi * 2 + core}
                ).wait_send()
        send_logits(hi).wait_send()
        send_tangents(hi).wait_send()
        send_exp(hi).wait_send()
        out_copy(hi).wait()
        cot_copy(hi).wait()


def local(n_dp, n_v, residual, norm_gain, gain_dir, head_weight, head_dir, sampled):
    n_hi = n_dp // 2
    rows, depth = residual.shape
    vocab = head_weight.shape[1]
    pad = -(-rows // 16) * 16
    f32, bf16 = jnp.float32, jnp.bfloat16
    vmem = pl.BlockSpec(memory_space=pltpu.VMEM)
    hbm = pl.BlockSpec(memory_space=pl.ANY)
    dma = pltpu.SemaphoreType.DMA
    pairs = [
        dma((n_dp, 2)), dma((n_dp, 2)),
        dma((n_hi, CHUNKS)), dma((n_hi, CHUNKS)), dma((n_hi, CHUNKS)), dma((n_hi, CHUNKS)),
        dma((n_hi,)), dma((n_hi,)), dma((n_hi,)), dma((n_hi,)), dma((n_hi,)), dma((n_hi,)),
        dma((1,)), dma((1,)), dma((n_v,)), dma((n_v,)), dma((n_dp, 2)), dma((n_dp, 2)),
        dma((n_v,)), dma((n_v,)), dma((n_dp,)), dma((n_dp,)),
    ]
    normed, cotangent, gain = pl.pallas_call(
        functools.partial(kernel, n_dp, n_v),
        out_shape=(
            jax.ShapeDtypeStruct((n_hi, 2 * pad, depth), bf16),
            jax.ShapeDtypeStruct((n_hi, 2 * pad, vocab), bf16),
            jax.ShapeDtypeStruct((1, depth), f32),
        ),
        in_specs=[vmem, vmem, vmem, vmem, hbm, hbm],
        out_specs=(hbm, hbm, vmem),
        scratch_shapes=[
            pltpu.VMEM((n_dp, CHUNKS, pad, depth // CHUNKS), bf16),
            pltpu.VMEM((depth, vocab), bf16),
            pltpu.VMEM((depth, vocab), bf16),
            pltpu.VMEM((n_hi, 2 * pad, depth), bf16),
            pltpu.VMEM((2 * pad, depth), bf16),
            pltpu.VMEM((2 * pad, depth), bf16),
            pltpu.VMEM((n_hi, 2, pad, vocab), f32),
            pltpu.VMEM((n_hi, 2, pad, vocab), f32),
            pltpu.VMEM((n_hi, pad, vocab), bf16),
            pltpu.VMEM((n_hi, rows, vocab), f32),
            pltpu.VMEM((n_hi, pad, vocab), bf16),
            pltpu.VMEM((n_hi, 2, pad, vocab), bf16),
            pltpu.VMEM((n_hi, 2 * pad, vocab), bf16),
            pltpu.VMEM((n_dp, 2, 1, LANES), f32),
            pltpu.VMEM((2, n_hi, 4, LANES), f32),
            pltpu.VMEM((n_v, n_hi, 4, LANES), f32),
            pltpu.VMEM((n_dp, 2, n_hi, 4, LANES), f32),
            pltpu.VMEM((n_v, 1, depth), f32),
            pltpu.VMEM((n_dp, 1, depth), f32),
            dma((2,)), dma((2, n_hi)),
        ] + pairs,
        compiler_params=pltpu.CompilerParams(
            collective_id=0, has_side_effects=True, vmem_limit_bytes=56 * MIB
        ),
        cost_estimate=pl.CostEstimate(
            flops=8 * n_dp * rows * depth * vocab,
            bytes_accessed=4 * depth * vocab,
            transcendentals=n_dp * rows * vocab,
        ),
    )(
        residual, norm_gain.reshape(1, depth), gain_dir.reshape(1, depth),
        sampled.reshape(1, -1), head_weight, head_dir,
    )
    product = lax.dot_general(
        normed.reshape(n_dp * pad, depth), cotangent.reshape(n_dp * pad, vocab),
        (((0,), (0,)), ((), ())), preferred_element_type=f32,
    )
    return norm_gain[:, None] * product, gain.reshape(depth)


def solution(mesh):
    assert mesh.shape["tensor"] == 2 and mesh.shape["dp"] % 2 == 0
    in_specs = (
        P("dp", "tensor"),
        P("tensor"),
        P("tensor"),
        P("tensor", ("dp", "vocab")),
        P("tensor", ("dp", "vocab")),
        P(),
    )
    out_specs = (P("tensor", ("dp", "vocab")), P("tensor"))
    return jax.shard_map(
        functools.partial(local, mesh.shape["dp"], mesh.shape["vocab"]),
        mesh=mesh, in_specs=in_specs, out_specs=out_specs, check_vma=False,
    )
```

```python
import functools

import jax
import jax.numpy as jnp
from jax import lax
from jax.experimental import pallas as pl
from jax.experimental.pallas import tpu as pltpu
from jax.sharding import PartitionSpec as P

EPSILON = 1e-06
LANES = 128
CHUNKS = 4
MIB = 1024 * 1024


def remote(src, dst, send_sem, recv_sem, device):
    return pltpu.make_async_remote_copy(
        src_ref=src,
        dst_ref=dst,
        send_sem=send_sem,
        recv_sem=recv_sem,
        device_id=device,
        device_id_type=pl.DeviceIdType.MESH,
    )


def merge(parts):
    top = functools.reduce(jnp.maximum, [part[0] for part in parts])
    scales = [jnp.exp(part[0] - top) for part in parts]
    total = sum(part[1] * scale for part, scale in zip(parts, scales))
    weighted = sum(part[2] * scale for part, scale in zip(parts, scales))
    picked = sum(part[3] for part in parts)
    return top, total, weighted, picked


def kernel(
    n_dp, n_v, res_ref, gain_ref, dir_ref, ids_ref, w_hbm, h_hbm, n_out, c_out, g_out,
    x, w, h, normed, turned, hid, tan, lg, tl, rl, eb, hot, co, na, nb, ss, ml, st, sz, sp, sc,
    gz, gp,
    in_sem, out_sem, ss_s, ss_r, xs_s, xs_r, cs_s, cs_r, ls_s, ls_r, es_s, es_r, ms_s, ms_r,
    sz_s, sz_r, sp_s, sp_r, gz_s, gz_r, gp_s, gp_r,
):
    n_hi = n_dp // 2
    rows, depth = res_ref.shape
    vocab = w.shape[1]
    pad = x.shape[2]
    width = x.shape[3]
    f32, bf16 = jnp.float32, jnp.bfloat16
    me, v, t = lax.axis_index("dp"), lax.axis_index("vocab"), lax.axis_index("tensor")
    core, my_hi = me % 2, me // 2
    other = 1 - t
    place = me * 2 + t
    mate = me + 1 - 2 * core
    core_peer, y_peer = {"dp": mate}, {"tensor": other}
    plane = [(place + k) % (2 * n_dp) for k in range(1, 2 * n_dp)]
    column = [(v + k) % n_v for k in range(1, n_v)]
    ring = [(me + k) % n_dp for k in range(1, n_dp)]

    barrier = pltpu.get_barrier_semaphore()
    for p in plane:
        pl.semaphore_signal(
            barrier, inc=1, device_id={"dp": p // 2, "tensor": p % 2},
            device_id_type=pl.DeviceIdType.MESH,
        )
    for z in column:
        pl.semaphore_signal(
            barrier, inc=1, device_id={"vocab": z}, device_id_type=pl.DeviceIdType.MESH
        )

    load_w = pltpu.make_async_copy(w_hbm, w, in_sem.at[0])
    load_h = pltpu.make_async_copy(h_hbm, h, in_sem.at[1])
    load_w.start()
    load_h.start()

    mask = lax.broadcasted_iota(jnp.int32, (pad, LANES), 0) == lax.broadcasted_iota(
        jnp.int32, (pad, LANES), 1
    )

    def to_row(col):
        return jnp.sum(jnp.where(mask, col, 0.0), axis=0, keepdims=True)

    def to_col(row):
        return jnp.sum(jnp.where(mask, row, 0.0), axis=1, keepdims=True)

    squares = jnp.zeros((pad, 1), f32)
    for c in range(CHUNKS):
        part = res_ref[:, c * width:(c + 1) * width].astype(f32)
        part = jnp.concatenate([part, jnp.zeros((pad - rows, width), f32)], axis=0)
        squares = squares + jnp.sum(part * part, axis=1, keepdims=True)
        x[me, c] = part.astype(bf16)
    ss[me, t] = to_row(squares)

    pl.semaphore_wait(barrier, len(plane) + len(column))

    for p in plane:
        remote(
            ss.at[me, t], ss.at[me, t], ss_s.at[p // 2, p % 2], ss_r.at[me, t],
            {"dp": p // 2, "tensor": p % 2},
        ).start()
    for c in range(CHUNKS):
        remote(x.at[me, c], x.at[me, c], cs_s.at[my_hi, c], cs_r.at[my_hi, c], core_peer).start()
    for c in range(CHUNKS):
        for k in range(1, n_hi):
            hi = (my_hi + k) % n_hi
            remote(
                x.at[me, c], x.at[me, c], xs_s.at[hi, c], xs_r.at[my_hi, c], {"dp": hi * 2 + core}
            ).start()

    def pass_on(hi, c):
        slot = x.at[hi * 2 + core, c]
        remote(slot, slot, xs_s.at[hi, c], xs_r.at[hi, c], {"dp": hi * 2 + core}).wait_recv()
        remote(slot, slot, cs_s.at[hi, c], cs_r.at[hi, c], core_peer).start()

    def wait_core(hi):
        for c in range(CHUNKS):
            slot = x.at[hi * 2 + 1 - core, c]
            remote(slot, slot, cs_s.at[hi, c], cs_r.at[hi, c], core_peer).wait_recv()

    for p in plane:
        slot = ss.at[p // 2, p % 2]
        remote(
            slot, slot, ss_s.at[p // 2, p % 2], ss_r.at[p // 2, p % 2],
            {"dp": p // 2, "tensor": p % 2},
        ).wait_recv()

    def out_copy(hi):
        return pltpu.make_async_copy(turned, n_out.at[hi], out_sem.at[0, hi])

    def cot_copy(hi):
        return pltpu.make_async_copy(co.at[hi], c_out.at[hi], out_sem.at[1, hi])

    def send_logits(hi):
        return remote(
            lg.at[hi, other, pl.ds(0, rows)], rl.at[hi], ls_s.at[hi], ls_r.at[hi], y_peer
        )

    def send_exp(hi):
        return remote(eb.at[hi, t], eb.at[hi, t], es_s.at[hi], es_r.at[hi], y_peer)

    def send_top(hi):
        return remote(ml.at[hi, t], ml.at[hi, t], ms_s.at[hi], ms_r.at[hi], y_peer)

    offset = (me * n_v + v) * vocab
    tokens = ids_ref.shape[0]

    def onehot(block):
        here = lax.broadcasted_iota(jnp.int32, (pad, tokens), 0)
        wanted = lax.broadcasted_iota(jnp.int32, (pad, tokens), 1) == here + block * rows
        ids = jnp.sum(
            jnp.where(wanted & (here < rows), ids_ref[...].reshape(1, tokens).astype(f32) + 1.0, 0.0),
            axis=1, keepdims=True,
        ).astype(jnp.int32) - 1
        return (lax.broadcasted_iota(jnp.int32, (pad, vocab), 1) == ids - offset).astype(f32)

    def pair(hi, first):
        inverse = jnp.concatenate(
            [
                to_col(lax.rsqrt((ss[hi * 2 + k, 0] + ss[hi * 2 + k, 1]) / (2 * depth) + EPSILON))
                for k in range(2)
            ],
            axis=0,
        )
        for c in range(CHUNKS):
            at = slice(c * width, (c + 1) * width)
            block = jnp.concatenate(
                [x[hi * 2, c].astype(f32), x[hi * 2 + 1, c].astype(f32)], axis=0
            )
            unit = (block * inverse).astype(bf16)
            normed[hi, :, at] = unit
            spread = unit.astype(f32)
            hid[:, at] = (spread * gain_ref[:, at]).astype(bf16)
            tan[:, at] = (spread * dir_ref[:, at]).astype(bf16)
        if first:
            load_w.wait()
        logits = jnp.dot(hid[...], w[...], preferred_element_type=f32)
        lg[hi, 0] = logits[:pad]
        lg[hi, 1] = logits[pad:]
        send_logits(hi).start()
        if first:
            load_h.wait()
        tangents = jnp.dot(hid[...], h[...], preferred_element_type=f32) + jnp.dot(
            tan[...], w[...], preferred_element_type=f32
        )
        tl[hi, 0] = tangents[:pad]
        tl[hi, 1] = tangents[pad:]
        hot[hi] = jnp.concatenate([onehot(hi * 2), onehot(hi * 2 + 1)], axis=0).astype(bf16)
        if not first:
            out_copy((hi + n_hi - 1) % n_hi).wait()
        turned[...] = normed[hi].T
        out_copy(hi).start()

    def finish(hi):
        send_logits(hi).wait_recv()
        blank = jnp.zeros((pad - rows, vocab), f32)
        logits = jnp.concatenate([lg[hi, t][:rows] + rl[hi], blank], axis=0)
        top = jnp.max(logits, axis=1, keepdims=True)
        eb[hi, t] = jnp.exp(logits - top).astype(bf16)
        ml[hi, t] = to_row(top)
        send_exp(hi).start()
        send_top(hi).start()

    def sums(hi, k):
        block = hi * 2 + k
        scaled, tangents = eb[hi, k].astype(f32), tl[hi, k]
        chosen = hot[hi, pl.ds(pl.multiple_of(k * pad, 16), pad)].astype(f32)
        at = pl.ds(block, 1)
        st[0, at] = ml[hi, k]
        st[1, at] = to_row(jnp.sum(scaled, axis=1, keepdims=True))
        st[2, at] = to_row(jnp.sum(scaled * tangents, axis=1, keepdims=True))
        st[3, at] = to_row(jnp.sum(chosen * tangents, axis=1, keepdims=True))

    def wait_exp(hi):
        slot = eb.at[hi, other]
        remote(slot, slot, es_s.at[hi], es_r.at[hi], y_peer).wait_recv()
        slot = ml.at[hi, other]
        remote(slot, slot, ms_s.at[hi], ms_r.at[hi], y_peer).wait_recv()

    def back(hi, k, carry=None):
        at = pl.ds(pl.multiple_of(k * pad, 16), pad)
        unit = normed[hi, at].astype(f32)
        turn = (((1,), (1,)), ((), ()))
        na[hi, k] = unit * lax.dot_general(hot[hi, at], w[...], turn, preferred_element_type=f32)
        nb[hi, k] = unit * lax.dot_general(eb[hi, k], w[...], turn, preferred_element_type=f32)

    wait_core(my_hi)
    pair(my_hi, True)

    def later(k, carry):
        hi = (my_hi + k) % n_hi
        for c in range(CHUNKS - 1):
            pass_on(hi, c)
        finish((my_hi + k - 1) % n_hi)
        pass_on(hi, CHUNKS - 1)
        wait_core(hi)
        pair(hi, False)
        return carry

    def early(k, carry):
        hi = (my_hi + k) % n_hi
        sums(hi, t)
        wait_exp(hi)
        sums(hi, other)
        return carry

    lax.fori_loop(1, n_hi, later, 0)
    last = (my_hi + n_hi - 1) % n_hi
    lax.fori_loop(0, n_hi - 1, early, 0)
    finish(last)
    sums(last, t)
    back(my_hi, t)
    wait_exp(last)
    sums(last, other)

    sz[v] = st[...]
    for z in column:
        remote(sz.at[v], sz.at[v], sz_s.at[z], sz_r.at[v], {"vocab": z}).start()
    back(my_hi, other)
    for z in column:
        remote(sz.at[z], sz.at[z], sz_s.at[z], sz_r.at[z], {"vocab": z}).wait_recv()
    joined = merge([[sz[z, i] for i in range(4)] for z in range(n_v)])
    for i in range(4):
        sp[me, t, i] = joined[i]
    for p in plane:
        remote(
            sp.at[me, t], sp.at[me, t], sp_s.at[p // 2, p % 2], sp_r.at[me, t],
            {"dp": p // 2, "tensor": p % 2},
        ).start()

    def rest(k, carry):
        hi = (my_hi + k) % n_hi
        back(hi, 0)
        back(hi, 1)
        return carry

    lax.fori_loop(1, n_hi, rest, 0)
    for p in plane:
        slot = sp.at[p // 2, p % 2]
        remote(
            slot, slot, sp_s.at[p // 2, p % 2], sp_r.at[p // 2, p % 2],
            {"dp": p // 2, "tensor": p % 2},
        ).wait_recv()
    top, total, weighted, picked = merge(
        [[sp[d, k, i] for i in range(4)] for d in range(n_dp) for k in range(2)]
    )
    total = 0.5 * total
    sc[0] = picked - weighted / total
    sc[1] = jnp.exp(st[0] - top) / total

    def gain_part(hi, grad):
        for k in range(2):
            at = pl.ds(hi * 2 + k, 1)
            score, factor = to_col(sc[0, at]), to_col(sc[1, at])
            grad = grad + jnp.sum(
                score * (na[hi, k] - factor * nb[hi, k]), axis=0, keepdims=True
            )
        return grad

    gz[v] = lax.fori_loop(0, n_hi, gain_part, jnp.zeros((1, depth), f32))
    for z in column:
        remote(gz.at[v], gz.at[v], gz_s.at[z], gz_r.at[v], {"vocab": z}).start()

    def cotangents(hi, carry):
        both = []
        for k in range(2):
            at = pl.ds(hi * 2 + k, 1)
            score, factor = to_col(sc[0, at]), to_col(sc[1, at])
            chosen = hot[hi, k * pad:(k + 1) * pad].astype(f32)
            both.append(score * (chosen - eb[hi, k].astype(f32) * factor))
        co[hi] = jnp.concatenate(both, axis=0).astype(bf16)
        cot_copy(hi).start()
        return carry

    lax.fori_loop(0, n_hi, cotangents, 0)
    for z in column:
        remote(gz.at[z], gz.at[z], gz_s.at[z], gz_r.at[z], {"vocab": z}).wait_recv()
    gp[me] = sum(gz[z] for z in range(n_v))
    for d in ring:
        remote(gp.at[me], gp.at[me], gp_s.at[d], gp_r.at[me], {"dp": d}).start()
    for d in ring:
        remote(gp.at[d], gp.at[d], gp_s.at[d], gp_r.at[d], {"dp": d}).wait_recv()
    g_out[...] = sum(gp[d] for d in range(n_dp))

    for p in plane:
        device = {"dp": p // 2, "tensor": p % 2}
        mine = ss.at[me, t]
        remote(mine, mine, ss_s.at[p // 2, p % 2], ss_r.at[me, t], device).wait_send()
        mine = sp.at[me, t]
        remote(mine, mine, sp_s.at[p // 2, p % 2], sp_r.at[me, t], device).wait_send()
    for z in column:
        remote(sz.at[v], sz.at[v], sz_s.at[z], sz_r.at[v], {"vocab": z}).wait_send()
        remote(gz.at[v], gz.at[v], gz_s.at[z], gz_r.at[v], {"vocab": z}).wait_send()
    for d in ring:
        remote(gp.at[me], gp.at[me], gp_s.at[d], gp_r.at[me], {"dp": d}).wait_send()
    for k in range(n_hi):
        hi = (my_hi + k) % n_hi
        for c in range(CHUNKS):
            mine = x.at[hi * 2 + core, c]
            remote(mine, mine, cs_s.at[hi, c], cs_r.at[hi, c], core_peer).wait_send()
            if k:
                mine = x.at[me, c]
                remote(
                    mine, mine, xs_s.at[hi, c], xs_r.at[my_hi, c], {"dp": hi * 2 + core}
                ).wait_send()
        send_logits(hi).wait_send()
        send_exp(hi).wait_send()
        send_top(hi).wait_send()
        cot_copy(hi).wait()
    out_copy(last).wait()


def last_kernel(turned, cot, gain_ref, sum_ref, head_ref, sum_out):
    tile = head_ref.shape[0]
    mask = lax.broadcasted_iota(jnp.int32, (tile, tile), 0) == lax.broadcasted_iota(
        jnp.int32, (tile, tile), 1
    )
    gain = jnp.sum(jnp.where(mask, gain_ref[...], 0.0), axis=1, keepdims=True)
    product = sum(
        jnp.dot(turned[hi], cot[hi], preferred_element_type=jnp.float32)
        for hi in range(turned.shape[0])
    )
    head_ref[...] = gain * product
    sum_out[...] = sum_ref[...]


def local(n_dp, n_v, residual, norm_gain, gain_dir, head_weight, head_dir, sampled):
    n_hi = n_dp // 2
    rows, depth = residual.shape
    vocab = head_weight.shape[1]
    pad = -(-rows // 16) * 16
    f32, bf16 = jnp.float32, jnp.bfloat16
    vmem = pl.BlockSpec(memory_space=pltpu.VMEM)
    hbm = pl.BlockSpec(memory_space=pl.ANY)
    dma = pltpu.SemaphoreType.DMA
    pairs = [
        dma((n_dp, 2)), dma((n_dp, 2)),
        dma((n_hi, CHUNKS)), dma((n_hi, CHUNKS)), dma((n_hi, CHUNKS)), dma((n_hi, CHUNKS)),
        dma((n_hi,)), dma((n_hi,)), dma((n_hi,)), dma((n_hi,)), dma((n_hi,)), dma((n_hi,)),
        dma((n_v,)), dma((n_v,)), dma((n_dp, 2)), dma((n_dp, 2)),
        dma((n_v,)), dma((n_v,)), dma((n_dp,)), dma((n_dp,)),
    ]
    gain_row = norm_gain.reshape(1, depth)
    turned, cotangent, gain = pl.pallas_call(
        functools.partial(kernel, n_dp, n_v),
        out_shape=(
            jax.ShapeDtypeStruct((n_hi, depth, 2 * pad), bf16),
            jax.ShapeDtypeStruct((n_hi, 2 * pad, vocab), bf16),
            jax.ShapeDtypeStruct((1, depth), f32),
        ),
        in_specs=[vmem, vmem, vmem, vmem, hbm, hbm],
        out_specs=(hbm, hbm, vmem),
        scratch_shapes=[
            pltpu.VMEM((n_dp, CHUNKS, pad, depth // CHUNKS), bf16),
            pltpu.VMEM((depth, vocab), bf16),
            pltpu.VMEM((depth, vocab), bf16),
            pltpu.VMEM((n_hi, 2 * pad, depth), bf16),
            pltpu.VMEM((depth, 2 * pad), bf16),
            pltpu.VMEM((2 * pad, depth), bf16),
            pltpu.VMEM((2 * pad, depth), bf16),
            pltpu.VMEM((n_hi, 2, pad, vocab), f32),
            pltpu.VMEM((n_hi, 2, pad, vocab), f32),
            pltpu.VMEM((n_hi, rows, vocab), f32),
            pltpu.VMEM((n_hi, 2, pad, vocab), bf16),
            pltpu.VMEM((n_hi, 2 * pad, vocab), bf16),
            pltpu.VMEM((n_hi, 2 * pad, vocab), bf16),
            pltpu.VMEM((n_hi, 2, pad, depth), f32),
            pltpu.VMEM((n_hi, 2, pad, depth), f32),
            pltpu.VMEM((n_dp, 2, 1, LANES), f32),
            pltpu.VMEM((n_hi, 2, 1, LANES), f32),
            pltpu.VMEM((4, n_dp, LANES), f32),
            pltpu.VMEM((n_v, 4, n_dp, LANES), f32),
            pltpu.VMEM((n_dp, 2, 4, n_dp, LANES), f32),
            pltpu.VMEM((2, n_dp, LANES), f32),
            pltpu.VMEM((n_v, 1, depth), f32),
            pltpu.VMEM((n_dp, 1, depth), f32),
            dma((2,)), dma((2, n_hi)),
        ] + pairs,
        compiler_params=pltpu.CompilerParams(
            collective_id=0, has_side_effects=True, vmem_limit_bytes=62 * MIB
        ),
        cost_estimate=pl.CostEstimate(
            flops=10 * n_dp * rows * depth * vocab,
            bytes_accessed=4 * depth * vocab,
            transcendentals=n_dp * rows * vocab,
        ),
    )(residual, gain_row, gain_dir.reshape(1, depth), sampled, head_weight, head_dir)
    tile = depth // 8
    fisher_head, fisher_gain = pl.pallas_call(
        last_kernel,
        grid=(depth // tile,),
        out_shape=(
            jax.ShapeDtypeStruct((depth, vocab), f32),
            jax.ShapeDtypeStruct((1, depth), f32),
        ),
        in_specs=[
            pl.BlockSpec((n_hi, tile, 2 * pad), lambda i: (0, i, 0)),
            pl.BlockSpec((n_hi, 2 * pad, vocab), lambda i: (0, 0, 0)),
            pl.BlockSpec((1, tile), lambda i: (0, i)),
            pl.BlockSpec((1, tile), lambda i: (0, i)),
        ],
        out_specs=(
            pl.BlockSpec((tile, vocab), lambda i: (i, 0)),
            pl.BlockSpec((1, tile), lambda i: (0, i)),
        ),
        compiler_params=pltpu.CompilerParams(vmem_limit_bytes=62 * MIB),
        cost_estimate=pl.CostEstimate(
            flops=2 * n_dp * rows * depth * vocab,
            bytes_accessed=4 * depth * vocab,
            transcendentals=0,
        ),
    )(turned, cotangent, gain_row, gain)
    return fisher_head, fisher_gain.reshape(depth)


def solution(mesh):
    assert mesh.shape["tensor"] == 2 and mesh.shape["dp"] % 2 == 0
    in_specs = (
        P("dp", "tensor"),
        P("tensor"),
        P("tensor"),
        P("tensor", ("dp", "vocab")),
        P("tensor", ("dp", "vocab")),
        P(),
    )
    out_specs = (P("tensor", ("dp", "vocab")), P("tensor"))
    return jax.shard_map(
        functools.partial(local, mesh.shape["dp"], mesh.shape["vocab"]),
        mesh=mesh, in_specs=in_specs, out_specs=out_specs, check_vma=False,
    )
```

```python
import functools

import jax
import jax.numpy as jnp
from jax import lax
from jax.experimental import pallas as pl
from jax.experimental.pallas import tpu as pltpu
from jax.sharding import PartitionSpec as P

EPSILON = 1e-06
LANES = 128
CHUNKS = 4
MIB = 1024 * 1024


def remote(src, dst, send_sem, recv_sem, device):
    return pltpu.make_async_remote_copy(
        src_ref=src,
        dst_ref=dst,
        send_sem=send_sem,
        recv_sem=recv_sem,
        device_id=device,
        device_id_type=pl.DeviceIdType.MESH,
    )


def merge(parts):
    top = functools.reduce(jnp.maximum, [part[0] for part in parts])
    scales = [jnp.exp(part[0] - top) for part in parts]
    total = sum(part[1] * scale for part, scale in zip(parts, scales))
    weighted = sum(part[2] * scale for part, scale in zip(parts, scales))
    picked = sum(part[3] for part in parts)
    return top, total, weighted, picked


def kernel(
    n_dp, n_v, res_ref, gain_ref, dir_ref, ids_ref, w_hbm, h_hbm, head_out, g_out,
    x, w, h, normed, hid, tan, lg, tl, rl, he, na, nb, stage, ss, ml, st, sz, sp, sc,
    gz, gp,
    in_sem, out_sem, ss_s, ss_r, xs_s, xs_r, zs_s, zs_r, cs_s, cs_r, ls_s, ls_r, es_s, es_r, ms_s, ms_r,
    sz_s, sz_r, sp_s, sp_r, gz_s, gz_r, gp_s, gp_r,
):
    n_hi = n_dp // 2
    rows, depth = res_ref.shape
    vocab = w.shape[1]
    pad = x.shape[2]
    width = x.shape[3]
    f32, bf16 = jnp.float32, jnp.bfloat16
    me, v, t = lax.axis_index("dp"), lax.axis_index("vocab"), lax.axis_index("tensor")
    core, my_hi = me % 2, me // 2
    other = 1 - t
    place = me * 2 + t
    mate = me + 1 - 2 * core
    core_peer, y_peer = {"dp": mate}, {"tensor": other}
    side = v % 2
    z_peer = {"vocab": v + 1 - 2 * side}
    half = CHUNKS // 2
    plane = [(place + k) % (2 * n_dp) for k in range(1, 2 * n_dp)]
    column = [(v + k) % n_v for k in range(1, n_v)]
    ring = [(me + k) % n_dp for k in range(1, n_dp)]

    barrier = pltpu.get_barrier_semaphore()
    for p in plane:
        pl.semaphore_signal(
            barrier, inc=1, device_id={"dp": p // 2, "tensor": p % 2},
            device_id_type=pl.DeviceIdType.MESH,
        )
    for z in column:
        pl.semaphore_signal(
            barrier, inc=1, device_id={"vocab": z}, device_id_type=pl.DeviceIdType.MESH
        )

    load_w = pltpu.make_async_copy(w_hbm, w, in_sem.at[0])
    load_h = pltpu.make_async_copy(h_hbm, h, in_sem.at[1])
    load_w.start()
    load_h.start()

    mask = lax.broadcasted_iota(jnp.int32, (pad, LANES), 0) == lax.broadcasted_iota(
        jnp.int32, (pad, LANES), 1
    )

    def to_row(col):
        return jnp.sum(jnp.where(mask, col, 0.0), axis=0, keepdims=True)

    def to_col(row):
        return jnp.sum(jnp.where(mask, row, 0.0), axis=1, keepdims=True)

    squares = jnp.zeros((pad, 1), f32)
    for c in range(CHUNKS):
        part = res_ref[:, c * width:(c + 1) * width].astype(f32)
        part = jnp.concatenate([part, jnp.zeros((pad - rows, width), f32)], axis=0)
        squares = squares + jnp.sum(part * part, axis=1, keepdims=True)
        x[me, c] = part.astype(bf16)
    ss[me, t] = to_row(squares)

    offset = (me * n_v + v) * vocab
    tokens = ids_ref.shape[0]

    def onehot(block):
        here = lax.broadcasted_iota(jnp.int32, (pad, tokens), 0)
        wanted = lax.broadcasted_iota(jnp.int32, (pad, tokens), 1) == here + block * rows
        ids = jnp.sum(
            jnp.where(wanted & (here < rows), ids_ref[...].reshape(1, tokens).astype(f32) + 1.0, 0.0),
            axis=1, keepdims=True,
        ).astype(jnp.int32) - 1
        return (lax.broadcasted_iota(jnp.int32, (pad, vocab), 1) == ids - offset).astype(
            f32
        ).astype(bf16)

    def mark(hi, carry):
        for k in range(2):
            he[hi, k] = onehot(hi * 2 + k)
        return carry

    pl.semaphore_wait(barrier, len(plane) + len(column))

    for p in plane:
        remote(
            ss.at[me, t], ss.at[me, t], ss_s.at[p // 2, p % 2], ss_r.at[me, t],
            {"dp": p // 2, "tensor": p % 2},
        ).start()
    for c in range(CHUNKS):
        remote(x.at[me, c], x.at[me, c], cs_s.at[my_hi, c], cs_r.at[my_hi, c], core_peer).start()
    def send_block(hi, j):
        c = side * half + j
        return remote(
            x.at[me, c], x.at[me, c], xs_s.at[hi, j], xs_r.at[my_hi, j], {"dp": hi * 2 + core}
        )

    def send_side(hi, j):
        slot = x.at[hi * 2 + core, side * half + j]
        return remote(slot, slot, zs_s.at[hi, j], zs_r.at[hi, j], z_peer)

    def send_core(hi, c):
        slot = x.at[hi * 2 + core, c]
        return remote(slot, slot, cs_s.at[hi, c], cs_r.at[hi, c], core_peer)

    for j in range(half):
        for k in range(1, n_hi):
            send_block((my_hi + k) % n_hi, j).start()

    def pass_on(hi, j):
        c = side * half + j
        slot = x.at[hi * 2 + core, c]
        remote(slot, slot, xs_s.at[hi, j], xs_r.at[hi, j], {"dp": hi * 2 + core}).wait_recv()
        send_side(hi, j).start()
        send_core(hi, c).start()

    def pass_side(hi, j):
        c = (1 - side) * half + j
        slot = x.at[hi * 2 + core, c]
        remote(slot, slot, zs_s.at[hi, j], zs_r.at[hi, j], z_peer).wait_recv()
        send_core(hi, c).start()

    def wait_core(hi):
        for c in range(CHUNKS):
            slot = x.at[hi * 2 + 1 - core, c]
            remote(slot, slot, cs_s.at[hi, c], cs_r.at[hi, c], core_peer).wait_recv()

    lax.fori_loop(0, n_hi, mark, 0)
    for p in plane:
        slot = ss.at[p // 2, p % 2]
        remote(
            slot, slot, ss_s.at[p // 2, p % 2], ss_r.at[p // 2, p % 2],
            {"dp": p // 2, "tensor": p % 2},
        ).wait_recv()

    def send_logits(hi):
        return remote(
            lg.at[hi, other, pl.ds(0, rows)], rl.at[hi], ls_s.at[hi], ls_r.at[hi], y_peer
        )

    def send_exp(hi):
        return remote(he.at[hi, 2 + t], he.at[hi, 2 + t], es_s.at[hi], es_r.at[hi], y_peer)

    def send_top(hi):
        return remote(ml.at[hi, t], ml.at[hi, t], ms_s.at[hi], ms_r.at[hi], y_peer)

    def pair(hi, first):
        inverse = jnp.concatenate(
            [
                to_col(lax.rsqrt((ss[hi * 2 + k, 0] + ss[hi * 2 + k, 1]) / (2 * depth) + EPSILON))
                for k in range(2)
            ],
            axis=0,
        )
        for c in range(CHUNKS):
            at = slice(c * width, (c + 1) * width)
            block = jnp.concatenate(
                [x[hi * 2, c].astype(f32), x[hi * 2 + 1, c].astype(f32)], axis=0
            )
            unit = (block * inverse).astype(bf16)
            normed[hi, :, at] = unit
            spread = unit.astype(f32)
            hid[:, at] = (spread * gain_ref[:, at]).astype(bf16)
            tan[:, at] = (spread * dir_ref[:, at]).astype(bf16)
        if first:
            load_w.wait()
        logits = jnp.dot(hid[...], w[...], preferred_element_type=f32)
        lg[hi, 0] = logits[:pad]
        lg[hi, 1] = logits[pad:]
        send_logits(hi).start()
        if first:
            load_h.wait()
        tangents = jnp.dot(hid[...], h[...], preferred_element_type=f32) + jnp.dot(
            tan[...], w[...], preferred_element_type=f32
        )
        tl[hi, 0] = tangents[:pad]
        tl[hi, 1] = tangents[pad:]

    def finish(hi):
        send_logits(hi).wait_recv()
        blank = jnp.zeros((pad - rows, vocab), f32)
        logits = jnp.concatenate([lg[hi, t][:rows] + rl[hi], blank], axis=0)
        top = jnp.max(logits, axis=1, keepdims=True)
        he[hi, 2 + t] = jnp.exp(logits - top).astype(bf16)
        ml[hi, t] = to_row(top)
        send_exp(hi).start()
        send_top(hi).start()

    def sums(hi, k):
        block = hi * 2 + k
        scaled, tangents = he[hi, 2 + k].astype(f32), tl[hi, k]
        chosen = he[hi, k].astype(f32)
        at = pl.ds(block, 1)
        st[0, at] = ml[hi, k]
        st[1, at] = to_row(jnp.sum(scaled, axis=1, keepdims=True))
        st[2, at] = to_row(jnp.sum(scaled * tangents, axis=1, keepdims=True))
        st[3, at] = to_row(jnp.sum(chosen * tangents, axis=1, keepdims=True))

    def wait_exp(hi):
        slot = he.at[hi, 2 + other]
        remote(slot, slot, es_s.at[hi], es_r.at[hi], y_peer).wait_recv()
        slot = ml.at[hi, other]
        remote(slot, slot, ms_s.at[hi], ms_r.at[hi], y_peer).wait_recv()

    def back(hi, part):
        at = slice(part * depth // 2, (part + 1) * depth // 2)
        both = jnp.concatenate([he[hi, k].astype(f32) for k in range(4)], axis=0).astype(bf16)
        turned = lax.dot_general(
            both, w[at], (((1,), (1,)), ((), ())), preferred_element_type=f32
        )
        unit = normed[hi, :, at].astype(f32)
        na[hi, :, at] = unit * turned[:2 * pad]
        nb[hi, :, at] = unit * turned[2 * pad:]

    wait_core(my_hi)
    pair(my_hi, True)

    def later(k, carry):
        hi = (my_hi + k) % n_hi
        for j in range(half):
            pass_on(hi, j)
        for j in range(half - 1):
            pass_side(hi, j)
        finish((my_hi + k - 1) % n_hi)
        pass_side(hi, half - 1)
        wait_core(hi)
        pair(hi, False)
        return carry

    def early(k, carry):
        hi = (my_hi + k) % n_hi
        sums(hi, t)
        wait_exp(hi)
        sums(hi, other)
        back(hi, 0)
        back(hi, 1)
        return carry

    lax.fori_loop(1, n_hi, later, 0)
    last = (my_hi + n_hi - 1) % n_hi
    lax.fori_loop(0, n_hi - 1, early, 0)
    finish(last)
    sums(last, t)
    wait_exp(last)
    sums(last, other)

    sz[v] = st[...]
    for z in column:
        remote(sz.at[v], sz.at[v], sz_s.at[z], sz_r.at[v], {"vocab": z}).start()
    back(last, 0)
    for z in column:
        remote(sz.at[z], sz.at[z], sz_s.at[z], sz_r.at[z], {"vocab": z}).wait_recv()
    joined = merge([[sz[z, i] for i in range(4)] for z in range(n_v)])
    for i in range(4):
        sp[me, t, i] = joined[i]
    for p in plane:
        remote(
            sp.at[me, t], sp.at[me, t], sp_s.at[p // 2, p % 2], sp_r.at[me, t],
            {"dp": p // 2, "tensor": p % 2},
        ).start()

    back(last, 1)
    for p in plane:
        slot = sp.at[p // 2, p % 2]
        remote(
            slot, slot, sp_s.at[p // 2, p % 2], sp_r.at[p // 2, p % 2],
            {"dp": p // 2, "tensor": p % 2},
        ).wait_recv()
    top, total, weighted, picked = merge(
        [[sp[d, k, i] for i in range(4)] for d in range(n_dp) for k in range(2)]
    )
    total = 0.5 * total
    sc[0] = picked - weighted / total
    sc[1] = jnp.exp(st[0] - top) / total

    def gain_part(hi, grad):
        for k in range(2):
            at, here = pl.ds(hi * 2 + k, 1), slice(k * pad, (k + 1) * pad)
            score, factor = to_col(sc[0, at]), to_col(sc[1, at])
            grad = grad + jnp.sum(
                score * (na[hi, here] - factor * nb[hi, here]), axis=0, keepdims=True
            )
        return grad

    gz[v] = lax.fori_loop(0, n_hi, gain_part, jnp.zeros((1, depth), f32))
    for z in column:
        remote(gz.at[v], gz.at[v], gz_s.at[z], gz_r.at[v], {"vocab": z}).start()

    def cotangents(hi, carry):
        for k in range(2):
            at = pl.ds(hi * 2 + k, 1)
            score, factor = to_col(sc[0, at]), to_col(sc[1, at])
            chosen = he[hi, k].astype(f32)
            he[hi, k] = (score * (chosen - he[hi, 2 + k].astype(f32) * factor)).astype(bf16)
        return carry

    lax.fori_loop(0, n_hi, cotangents, 0)

    slots, tile = stage.shape[0], stage.shape[1]
    tiles = depth // tile
    square = lax.broadcasted_iota(jnp.int32, (tile, tile), 0) == lax.broadcasted_iota(
        jnp.int32, (tile, tile), 1
    )

    def head_copy(i):
        return pltpu.make_async_copy(
            stage.at[i % slots], head_out.at[pl.ds(i * tile, tile)], out_sem.at[i % slots]
        )

    def head_tile(i):
        at = slice(i * tile, (i + 1) * tile)
        product = sum(
            lax.dot_general(
                normed[hi, :, at], he[hi, 0:2].reshape(2 * pad, vocab), (((0,), (0,)), ((), ())),
                preferred_element_type=f32,
            )
            for hi in range(n_hi)
        )
        if i >= slots:
            head_copy(i - slots).wait()
        gain = jnp.sum(jnp.where(square, gain_ref[:, at], 0.0), axis=1, keepdims=True)
        stage[i % slots] = gain * product
        head_copy(i).start()

    for i in range(tiles // 2):
        head_tile(i)
    for z in column:
        remote(gz.at[z], gz.at[z], gz_s.at[z], gz_r.at[z], {"vocab": z}).wait_recv()
    gp[me] = sum(gz[z] for z in range(n_v))
    for d in ring:
        remote(gp.at[me], gp.at[me], gp_s.at[d], gp_r.at[me], {"dp": d}).start()
    for i in range(tiles // 2, tiles):
        head_tile(i)
    for d in ring:
        remote(gp.at[d], gp.at[d], gp_s.at[d], gp_r.at[d], {"dp": d}).wait_recv()
    g_out[...] = sum(gp[d] for d in range(n_dp))

    for p in plane:
        device = {"dp": p // 2, "tensor": p % 2}
        mine = ss.at[me, t]
        remote(mine, mine, ss_s.at[p // 2, p % 2], ss_r.at[me, t], device).wait_send()
        mine = sp.at[me, t]
        remote(mine, mine, sp_s.at[p // 2, p % 2], sp_r.at[me, t], device).wait_send()
    for z in column:
        remote(sz.at[v], sz.at[v], sz_s.at[z], sz_r.at[v], {"vocab": z}).wait_send()
        remote(gz.at[v], gz.at[v], gz_s.at[z], gz_r.at[v], {"vocab": z}).wait_send()
    for d in ring:
        remote(gp.at[me], gp.at[me], gp_s.at[d], gp_r.at[me], {"dp": d}).wait_send()
    for k in range(n_hi):
        hi = (my_hi + k) % n_hi
        for c in range(CHUNKS):
            send_core(hi, c).wait_send()
        if k:
            for j in range(half):
                send_block(hi, j).wait_send()
                send_side(hi, j).wait_send()
        send_logits(hi).wait_send()
        send_exp(hi).wait_send()
        send_top(hi).wait_send()
    for i in range(max(tiles - slots, 0), tiles):
        head_copy(i).wait()


def local(n_dp, n_v, residual, norm_gain, gain_dir, head_weight, head_dir, sampled):
    n_hi = n_dp // 2
    rows, depth = residual.shape
    vocab = head_weight.shape[1]
    pad = -(-rows // 16) * 16
    f32, bf16 = jnp.float32, jnp.bfloat16
    vmem = pl.BlockSpec(memory_space=pltpu.VMEM)
    hbm = pl.BlockSpec(memory_space=pl.ANY)
    dma = pltpu.SemaphoreType.DMA
    pairs = [
        dma((n_dp, 2)), dma((n_dp, 2)),
        dma((n_hi, CHUNKS)), dma((n_hi, CHUNKS)), dma((n_hi, CHUNKS)), dma((n_hi, CHUNKS)),
        dma((n_hi, CHUNKS)), dma((n_hi, CHUNKS)),
        dma((n_hi,)), dma((n_hi,)), dma((n_hi,)), dma((n_hi,)), dma((n_hi,)), dma((n_hi,)),
        dma((n_v,)), dma((n_v,)), dma((n_dp, 2)), dma((n_dp, 2)),
        dma((n_v,)), dma((n_v,)), dma((n_dp,)), dma((n_dp,)),
    ]
    tile = depth // 8
    slots = 4 if n_dp <= 4 else 2
    fisher_head, fisher_gain = pl.pallas_call(
        functools.partial(kernel, n_dp, n_v),
        out_shape=(
            jax.ShapeDtypeStruct((depth, vocab), f32),
            jax.ShapeDtypeStruct((1, depth), f32),
        ),
        in_specs=[vmem, vmem, vmem, vmem] + [hbm, hbm],
        out_specs=(hbm, vmem),
        scratch_shapes=[
            pltpu.VMEM((n_dp, CHUNKS, pad, depth // CHUNKS), bf16),
            pltpu.VMEM((depth, vocab), bf16),
            pltpu.VMEM((depth, vocab), bf16),
            pltpu.VMEM((n_hi, 2 * pad, depth), bf16),
            pltpu.VMEM((2 * pad, depth), bf16),
            pltpu.VMEM((2 * pad, depth), bf16),
            pltpu.VMEM((n_hi, 2, pad, vocab), f32),
            pltpu.VMEM((n_hi, 2, pad, vocab), f32),
            pltpu.VMEM((n_hi, rows, vocab), f32),
            pltpu.VMEM((n_hi, 4, pad, vocab), bf16),
            pltpu.VMEM((n_hi, 2 * pad, depth), f32),
            pltpu.VMEM((n_hi, 2 * pad, depth), f32),
            pltpu.VMEM((slots, tile, vocab), f32),
            pltpu.VMEM((n_dp, 2, 1, LANES), f32),
            pltpu.VMEM((n_hi, 2, 1, LANES), f32),
            pltpu.VMEM((4, n_dp, LANES), f32),
            pltpu.VMEM((n_v, 4, n_dp, LANES), f32),
            pltpu.VMEM((n_dp, 2, 4, n_dp, LANES), f32),
            pltpu.VMEM((2, n_dp, LANES), f32),
            pltpu.VMEM((n_v, 1, depth), f32),
            pltpu.VMEM((n_dp, 1, depth), f32),
            dma((2,)), dma((slots,)),
        ] + pairs,
        compiler_params=pltpu.CompilerParams(
            collective_id=0, has_side_effects=True, vmem_limit_bytes=(36 if n_dp <= 4 else 62) * MIB
        ),
        cost_estimate=pl.CostEstimate(
            flops=10 * n_dp * rows * depth * vocab,
            bytes_accessed=4 * depth * vocab,
            transcendentals=n_dp * rows * vocab,
        ),
    )(residual, norm_gain.reshape(1, depth), gain_dir.reshape(1, depth), sampled, head_weight, head_dir)
    return fisher_head, fisher_gain.reshape(depth)


def solution(mesh):
    assert mesh.shape["tensor"] == 2 and mesh.shape["dp"] % 2 == 0
    in_specs = (
        P("dp", "tensor"),
        P("tensor"),
        P("tensor"),
        P("tensor", ("dp", "vocab")),
        P("tensor", ("dp", "vocab")),
        P(),
    )
    out_specs = (P("tensor", ("dp", "vocab")), P("tensor"))
    return jax.shard_map(
        functools.partial(local, mesh.shape["dp"], mesh.shape["vocab"]),
        mesh=mesh, in_specs=in_specs, out_specs=out_specs, check_vma=False,
    )
```

```python
import functools

import jax
import jax.numpy as jnp
from jax import lax
from jax.experimental import pallas as pl
from jax.experimental.pallas import tpu as pltpu
from jax.sharding import PartitionSpec as P

EPSILON = 1e-06
LANES = 128
CHUNKS = 4
MIB = 1024 * 1024


def remote(src, dst, send_sem, recv_sem, device):
    return pltpu.make_async_remote_copy(
        src_ref=src,
        dst_ref=dst,
        send_sem=send_sem,
        recv_sem=recv_sem,
        device_id=device,
        device_id_type=pl.DeviceIdType.MESH,
    )


def merge(parts):
    top = functools.reduce(jnp.maximum, [part[0] for part in parts])
    scales = [jnp.exp(part[0] - top) for part in parts]
    total = sum(part[1] * scale for part, scale in zip(parts, scales))
    weighted = sum(part[2] * scale for part, scale in zip(parts, scales))
    picked = sum(part[3] for part in parts)
    return top, total, weighted, picked


def kernel(
    n_dp, n_v, res_ref, gain_ref, dir_ref, ids_ref, w_hbm, h_hbm, head_out, g_out,
    x, w, h, normed, hid, tan, lg, tl, rl, he, na, nb, stage, ss, ml, st, sz, sp, sc,
    gz, gp,
    in_sem, out_sem, ss_s, ss_r, xs_s, xs_r, zs_s, zs_r, cs_s, cs_r, ls_s, ls_r, es_s, es_r, ms_s, ms_r,
    sz_s, sz_r, sp_s, sp_r, gz_s, gz_r, gp_s, gp_r,
):
    n_hi = n_dp // 2
    rows, depth = res_ref.shape
    vocab = w.shape[1]
    pad = x.shape[2]
    width = x.shape[3]
    f32, bf16 = jnp.float32, jnp.bfloat16
    me, v, t = lax.axis_index("dp"), lax.axis_index("vocab"), lax.axis_index("tensor")
    core, my_hi = me % 2, me // 2
    other = 1 - t
    place = me * 2 + t
    mate = me + 1 - 2 * core
    core_peer, y_peer = {"dp": mate}, {"tensor": other}
    side = v % 2
    z_peer = {"vocab": v + 1 - 2 * side}
    half = CHUNKS // 2
    plane = [(place + k) % (2 * n_dp) for k in range(1, 2 * n_dp)]
    column = [(v + k) % n_v for k in range(1, n_v)]
    ring = [(me + k) % n_dp for k in range(1, n_dp)]

    barrier = pltpu.get_barrier_semaphore()
    for p in plane:
        pl.semaphore_signal(
            barrier, inc=1, device_id={"dp": p // 2, "tensor": p % 2},
            device_id_type=pl.DeviceIdType.MESH,
        )
    for z in column:
        pl.semaphore_signal(
            barrier, inc=1, device_id={"vocab": z}, device_id_type=pl.DeviceIdType.MESH
        )

    load_w = pltpu.make_async_copy(w_hbm, w, in_sem.at[0])
    load_h = pltpu.make_async_copy(h_hbm, h, in_sem.at[1])
    load_w.start()
    load_h.start()

    mask = lax.broadcasted_iota(jnp.int32, (pad, LANES), 0) == lax.broadcasted_iota(
        jnp.int32, (pad, LANES), 1
    )

    def to_row(col):
        return jnp.sum(jnp.where(mask, col, 0.0), axis=0, keepdims=True)

    def to_col(row):
        return jnp.sum(jnp.where(mask, row, 0.0), axis=1, keepdims=True)

    squares = jnp.zeros((pad, 1), f32)
    for c in range(CHUNKS):
        part = res_ref[:, c * width:(c + 1) * width].astype(f32)
        part = jnp.concatenate([part, jnp.zeros((pad - rows, width), f32)], axis=0)
        squares = squares + jnp.sum(part * part, axis=1, keepdims=True)
        x[me, c] = part.astype(bf16)
    ss[me, t] = to_row(squares)

    offset = (me * n_v + v) * vocab
    tokens = ids_ref.shape[0]

    def onehot(block):
        here = lax.broadcasted_iota(jnp.int32, (pad, tokens), 0)
        wanted = lax.broadcasted_iota(jnp.int32, (pad, tokens), 1) == here + block * rows
        ids = jnp.sum(
            jnp.where(wanted & (here < rows), ids_ref[...].reshape(1, tokens).astype(f32) + 1.0, 0.0),
            axis=1, keepdims=True,
        ).astype(jnp.int32) - 1
        return (lax.broadcasted_iota(jnp.int32, (pad, vocab), 1) == ids - offset).astype(
            f32
        ).astype(bf16)

    def mark(hi, carry):
        for k in range(2):
            he[hi, k] = onehot(hi * 2 + k)
        return carry

    pl.semaphore_wait(barrier, len(plane) + len(column))

    for p in plane:
        remote(
            ss.at[me, t], ss.at[me, t], ss_s.at[p // 2, p % 2], ss_r.at[me, t],
            {"dp": p // 2, "tensor": p % 2},
        ).start()
    for c in range(CHUNKS):
        remote(x.at[me, c], x.at[me, c], cs_s.at[my_hi, c], cs_r.at[my_hi, c], core_peer).start()
    def send_block(hi, j):
        c = side * half + j
        return remote(
            x.at[me, c], x.at[me, c], xs_s.at[hi, j], xs_r.at[my_hi, j], {"dp": hi * 2 + core}
        )

    def send_side(hi, j):
        slot = x.at[hi * 2 + core, side * half + j]
        return remote(slot, slot, zs_s.at[hi, j], zs_r.at[hi, j], z_peer)

    def send_core(hi, c):
        slot = x.at[hi * 2 + core, c]
        return remote(slot, slot, cs_s.at[hi, c], cs_r.at[hi, c], core_peer)

    for j in range(half):
        for k in range(1, n_hi):
            send_block((my_hi + k) % n_hi, j).start()

    def pass_on(hi, j):
        c = side * half + j
        slot = x.at[hi * 2 + core, c]
        remote(slot, slot, xs_s.at[hi, j], xs_r.at[hi, j], {"dp": hi * 2 + core}).wait_recv()
        send_side(hi, j).start()
        send_core(hi, c).start()

    def pass_side(hi, j):
        c = (1 - side) * half + j
        slot = x.at[hi * 2 + core, c]
        remote(slot, slot, zs_s.at[hi, j], zs_r.at[hi, j], z_peer).wait_recv()
        send_core(hi, c).start()

    def wait_core(hi):
        for c in range(CHUNKS):
            slot = x.at[hi * 2 + 1 - core, c]
            remote(slot, slot, cs_s.at[hi, c], cs_r.at[hi, c], core_peer).wait_recv()

    lax.fori_loop(0, n_hi, mark, 0)
    for p in plane:
        slot = ss.at[p // 2, p % 2]
        remote(
            slot, slot, ss_s.at[p // 2, p % 2], ss_r.at[p // 2, p % 2],
            {"dp": p // 2, "tensor": p % 2},
        ).wait_recv()

    def send_logits(hi):
        return remote(
            lg.at[hi, other, pl.ds(0, rows)], rl.at[hi], ls_s.at[hi], ls_r.at[hi], y_peer
        )

    def send_exp(hi):
        return remote(he.at[hi, 2 + t], he.at[hi, 2 + t], es_s.at[hi], es_r.at[hi], y_peer)

    def send_top(hi):
        return remote(ml.at[hi, t], ml.at[hi, t], ms_s.at[hi], ms_r.at[hi], y_peer)

    def pair(hi, first):
        inverse = jnp.concatenate(
            [
                to_col(lax.rsqrt((ss[hi * 2 + k, 0] + ss[hi * 2 + k, 1]) / (2 * depth) + EPSILON))
                for k in range(2)
            ],
            axis=0,
        )
        for c in range(CHUNKS):
            at = slice(c * width, (c + 1) * width)
            block = jnp.concatenate(
                [x[hi * 2, c].astype(f32), x[hi * 2 + 1, c].astype(f32)], axis=0
            )
            unit = (block * inverse).astype(bf16)
            normed[hi, :, at] = unit
            spread = unit.astype(f32)
            hid[:, at] = (spread * gain_ref[:, at]).astype(bf16)
            tan[:, at] = (spread * dir_ref[:, at]).astype(bf16)
        if first:
            load_w.wait()
        logits = jnp.dot(hid[...], w[...], preferred_element_type=f32)
        lg[hi, 0] = logits[:pad]
        lg[hi, 1] = logits[pad:]
        send_logits(hi).start()
        if first:
            load_h.wait()
        tangents = jnp.dot(hid[...], h[...], preferred_element_type=f32) + jnp.dot(
            tan[...], w[...], preferred_element_type=f32
        )
        tl[hi, 0] = tangents[:pad]
        tl[hi, 1] = tangents[pad:]

    def finish(hi):
        send_logits(hi).wait_recv()
        blank = jnp.zeros((pad - rows, vocab), f32)
        logits = jnp.concatenate([lg[hi, t][:rows] + rl[hi], blank], axis=0)
        top = jnp.max(logits, axis=1, keepdims=True)
        he[hi, 2 + t] = jnp.exp(logits - top).astype(bf16)
        ml[hi, t] = to_row(top)
        send_exp(hi).start()
        send_top(hi).start()

    def sums(hi, k):
        block = hi * 2 + k
        scaled, tangents = he[hi, 2 + k].astype(f32), tl[hi, k]
        chosen = he[hi, k].astype(f32)
        at = pl.ds(block, 1)
        st[0, at] = ml[hi, k]
        st[1, at] = to_row(jnp.sum(scaled, axis=1, keepdims=True))
        st[2, at] = to_row(jnp.sum(scaled * tangents, axis=1, keepdims=True))
        st[3, at] = to_row(jnp.sum(chosen * tangents, axis=1, keepdims=True))

    def wait_exp(hi):
        slot = he.at[hi, 2 + other]
        remote(slot, slot, es_s.at[hi], es_r.at[hi], y_peer).wait_recv()
        slot = ml.at[hi, other]
        remote(slot, slot, ms_s.at[hi], ms_r.at[hi], y_peer).wait_recv()

    def back(hi, part):
        at = slice(part * depth // 2, (part + 1) * depth // 2)
        both = jnp.concatenate([he[hi, k].astype(f32) for k in range(4)], axis=0).astype(bf16)
        turned = lax.dot_general(
            both, w[at], (((1,), (1,)), ((), ())), preferred_element_type=f32
        )
        unit = normed[hi, :, at].astype(f32)
        na[hi, :, at] = unit * turned[:2 * pad]
        nb[hi, :, at] = unit * turned[2 * pad:]

    wait_core(my_hi)
    pair(my_hi, True)

    def later(k, carry):
        hi = (my_hi + k) % n_hi
        for j in range(half):
            pass_on(hi, j)
        for j in range(half):
            pass_side(hi, j)
        wait_core(hi)
        pair(hi, False)
        finish((my_hi + k - 1) % n_hi)
        return carry

    def early(k, carry):
        hi = (my_hi + k) % n_hi
        sums(hi, t)
        wait_exp(hi)
        sums(hi, other)
        back(hi, 0)
        back(hi, 1)
        return carry

    lax.fori_loop(1, n_hi, later, 0)
    last = (my_hi + n_hi - 1) % n_hi
    lax.fori_loop(0, n_hi - 1, early, 0)
    finish(last)
    sums(last, t)
    wait_exp(last)
    sums(last, other)

    sz[v] = st[...]
    for z in column:
        remote(sz.at[v], sz.at[v], sz_s.at[z], sz_r.at[v], {"vocab": z}).start()
    back(last, 0)
    for z in column:
        remote(sz.at[z], sz.at[z], sz_s.at[z], sz_r.at[z], {"vocab": z}).wait_recv()
    joined = merge([[sz[z, i] for i in range(4)] for z in range(n_v)])
    for i in range(4):
        sp[me, t, i] = joined[i]
    for p in plane:
        remote(
            sp.at[me, t], sp.at[me, t], sp_s.at[p // 2, p % 2], sp_r.at[me, t],
            {"dp": p // 2, "tensor": p % 2},
        ).start()

    back(last, 1)
    for p in plane:
        slot = sp.at[p // 2, p % 2]
        remote(
            slot, slot, sp_s.at[p // 2, p % 2], sp_r.at[p // 2, p % 2],
            {"dp": p // 2, "tensor": p % 2},
        ).wait_recv()
    top, total, weighted, picked = merge(
        [[sp[d, k, i] for i in range(4)] for d in range(n_dp) for k in range(2)]
    )
    total = 0.5 * total
    sc[0] = picked - weighted / total
    sc[1] = jnp.exp(st[0] - top) / total

    def gain_part(hi, grad):
        for k in range(2):
            at, here = pl.ds(hi * 2 + k, 1), slice(k * pad, (k + 1) * pad)
            score, factor = to_col(sc[0, at]), to_col(sc[1, at])
            grad = grad + jnp.sum(
                score * (na[hi, here] - factor * nb[hi, here]), axis=0, keepdims=True
            )
        return grad

    gz[v] = lax.fori_loop(0, n_hi, gain_part, jnp.zeros((1, depth), f32))
    for z in column:
        remote(gz.at[v], gz.at[v], gz_s.at[z], gz_r.at[v], {"vocab": z}).start()

    def cotangents(hi, carry):
        for k in range(2):
            at = pl.ds(hi * 2 + k, 1)
            score, factor = to_col(sc[0, at]), to_col(sc[1, at])
            chosen = he[hi, k].astype(f32)
            he[hi, k] = (score * (chosen - he[hi, 2 + k].astype(f32) * factor)).astype(bf16)
        return carry

    lax.fori_loop(0, n_hi, cotangents, 0)

    slots, tile = stage.shape[0], stage.shape[1]
    tiles = depth // tile
    square = lax.broadcasted_iota(jnp.int32, (tile, tile), 0) == lax.broadcasted_iota(
        jnp.int32, (tile, tile), 1
    )

    def head_copy(i):
        return pltpu.make_async_copy(
            stage.at[i % slots], head_out.at[pl.ds(i * tile, tile)], out_sem.at[i % slots]
        )

    def head_tile(i):
        at = slice(i * tile, (i + 1) * tile)
        product = sum(
            lax.dot_general(
                normed[hi, :, at], he[hi, 0:2].reshape(2 * pad, vocab), (((0,), (0,)), ((), ())),
                preferred_element_type=f32,
            )
            for hi in range(n_hi)
        )
        if i >= slots:
            head_copy(i - slots).wait()
        gain = jnp.sum(jnp.where(square, gain_ref[:, at], 0.0), axis=1, keepdims=True)
        stage[i % slots] = gain * product
        head_copy(i).start()

    for i in range(tiles // 2):
        head_tile(i)
    for z in column:
        remote(gz.at[z], gz.at[z], gz_s.at[z], gz_r.at[z], {"vocab": z}).wait_recv()
    gp[me] = sum(gz[z] for z in range(n_v))
    for d in ring:
        remote(gp.at[me], gp.at[me], gp_s.at[d], gp_r.at[me], {"dp": d}).start()
    for i in range(tiles // 2, tiles):
        head_tile(i)
    for d in ring:
        remote(gp.at[d], gp.at[d], gp_s.at[d], gp_r.at[d], {"dp": d}).wait_recv()
    g_out[...] = sum(gp[d] for d in range(n_dp))

    for p in plane:
        device = {"dp": p // 2, "tensor": p % 2}
        mine = ss.at[me, t]
        remote(mine, mine, ss_s.at[p // 2, p % 2], ss_r.at[me, t], device).wait_send()
        mine = sp.at[me, t]
        remote(mine, mine, sp_s.at[p // 2, p % 2], sp_r.at[me, t], device).wait_send()
    for z in column:
        remote(sz.at[v], sz.at[v], sz_s.at[z], sz_r.at[v], {"vocab": z}).wait_send()
        remote(gz.at[v], gz.at[v], gz_s.at[z], gz_r.at[v], {"vocab": z}).wait_send()
    for d in ring:
        remote(gp.at[me], gp.at[me], gp_s.at[d], gp_r.at[me], {"dp": d}).wait_send()
    for k in range(n_hi):
        hi = (my_hi + k) % n_hi
        for c in range(CHUNKS):
            send_core(hi, c).wait_send()
        if k:
            for j in range(half):
                send_block(hi, j).wait_send()
                send_side(hi, j).wait_send()
        send_logits(hi).wait_send()
        send_exp(hi).wait_send()
        send_top(hi).wait_send()
    for i in range(max(tiles - slots, 0), tiles):
        head_copy(i).wait()


def local(n_dp, n_v, residual, norm_gain, gain_dir, head_weight, head_dir, sampled):
    n_hi = n_dp // 2
    rows, depth = residual.shape
    vocab = head_weight.shape[1]
    pad = -(-rows // 16) * 16
    f32, bf16 = jnp.float32, jnp.bfloat16
    vmem = pl.BlockSpec(memory_space=pltpu.VMEM)
    hbm = pl.BlockSpec(memory_space=pl.ANY)
    dma = pltpu.SemaphoreType.DMA
    pairs = [
        dma((n_dp, 2)), dma((n_dp, 2)),
        dma((n_hi, CHUNKS)), dma((n_hi, CHUNKS)), dma((n_hi, CHUNKS)), dma((n_hi, CHUNKS)),
        dma((n_hi, CHUNKS)), dma((n_hi, CHUNKS)),
        dma((n_hi,)), dma((n_hi,)), dma((n_hi,)), dma((n_hi,)), dma((n_hi,)), dma((n_hi,)),
        dma((n_v,)), dma((n_v,)), dma((n_dp, 2)), dma((n_dp, 2)),
        dma((n_v,)), dma((n_v,)), dma((n_dp,)), dma((n_dp,)),
    ]
    tile = depth // 8
    slots = 4 if n_dp <= 4 else 2
    fisher_head, fisher_gain = pl.pallas_call(
        functools.partial(kernel, n_dp, n_v),
        out_shape=(
            jax.ShapeDtypeStruct((depth, vocab), f32),
            jax.ShapeDtypeStruct((1, depth), f32),
        ),
        in_specs=[vmem, vmem, vmem, vmem] + [hbm, hbm],
        out_specs=(hbm, vmem),
        scratch_shapes=[
            pltpu.VMEM((n_dp, CHUNKS, pad, depth // CHUNKS), bf16),
            pltpu.VMEM((depth, vocab), bf16),
            pltpu.VMEM((depth, vocab), bf16),
            pltpu.VMEM((n_hi, 2 * pad, depth), bf16),
            pltpu.VMEM((2 * pad, depth), bf16),
            pltpu.VMEM((2 * pad, depth), bf16),
            pltpu.VMEM((n_hi, 2, pad, vocab), f32),
            pltpu.VMEM((n_hi, 2, pad, vocab), f32),
            pltpu.VMEM((n_hi, rows, vocab), f32),
            pltpu.VMEM((n_hi, 4, pad, vocab), bf16),
            pltpu.VMEM((n_hi, 2 * pad, depth), f32),
            pltpu.VMEM((n_hi, 2 * pad, depth), f32),
            pltpu.VMEM((slots, tile, vocab), f32),
            pltpu.VMEM((n_dp, 2, 1, LANES), f32),
            pltpu.VMEM((n_hi, 2, 1, LANES), f32),
            pltpu.VMEM((4, n_dp, LANES), f32),
            pltpu.VMEM((n_v, 4, n_dp, LANES), f32),
            pltpu.VMEM((n_dp, 2, 4, n_dp, LANES), f32),
            pltpu.VMEM((2, n_dp, LANES), f32),
            pltpu.VMEM((n_v, 1, depth), f32),
            pltpu.VMEM((n_dp, 1, depth), f32),
            dma((2,)), dma((slots,)),
        ] + pairs,
        compiler_params=pltpu.CompilerParams(
            collective_id=0, has_side_effects=True, vmem_limit_bytes=62 * MIB
        ),
        cost_estimate=pl.CostEstimate(
            flops=10 * n_dp * rows * depth * vocab,
            bytes_accessed=4 * depth * vocab,
            transcendentals=n_dp * rows * vocab,
        ),
    )(residual, norm_gain.reshape(1, depth), gain_dir.reshape(1, depth), sampled, head_weight, head_dir)
    return fisher_head, fisher_gain.reshape(depth)


def solution(mesh):
    assert mesh.shape["tensor"] == 2 and mesh.shape["dp"] % 2 == 0
    in_specs = (
        P("dp", "tensor"),
        P("tensor"),
        P("tensor"),
        P("tensor", ("dp", "vocab")),
        P("tensor", ("dp", "vocab")),
        P(),
    )
    out_specs = (P("tensor", ("dp", "vocab")), P("tensor"))
    return jax.shard_map(
        functools.partial(local, mesh.shape["dp"], mesh.shape["vocab"]),
        mesh=mesh, in_specs=in_specs, out_specs=out_specs, check_vma=False,
    )
```

```python
import functools

import jax
import jax.numpy as jnp
from jax import lax
from jax.experimental import pallas as pl
from jax.experimental.pallas import tpu as pltpu
from jax.sharding import PartitionSpec as P

EPSILON = 1e-06
LANES = 128
CHUNKS = 4
MIB = 1024 * 1024


def remote(src, dst, send_sem, recv_sem, device):
    return pltpu.make_async_remote_copy(
        src_ref=src,
        dst_ref=dst,
        send_sem=send_sem,
        recv_sem=recv_sem,
        device_id=device,
        device_id_type=pl.DeviceIdType.MESH,
    )


def merge(parts):
    top = functools.reduce(jnp.maximum, [part[0] for part in parts])
    scales = [jnp.exp(part[0] - top) for part in parts]
    total = sum(part[1] * scale for part, scale in zip(parts, scales))
    weighted = sum(part[2] * scale for part, scale in zip(parts, scales))
    picked = sum(part[3] for part in parts)
    return top, total, weighted, picked


def kernel(
    n_dp, n_v, res_ref, gain_ref, dir_ref, ids_ref, w_hbm, h_hbm, n_out, c_out, g_out,
    x, w, h, normed, hid, tan, lg, tl, rl, he, na, nb, ss, ml, st, sz, sp, sc,
    gz, gp,
    in_sem, out_sem, ss_s, ss_r, xs_s, xs_r, zs_s, zs_r, cs_s, cs_r, ls_s, ls_r, es_s, es_r, ms_s, ms_r,
    sz_s, sz_r, sp_s, sp_r, gz_s, gz_r, gp_s, gp_r,
):
    n_hi = n_dp // 2
    rows, depth = res_ref.shape
    vocab = w.shape[1]
    pad = x.shape[2]
    width = x.shape[3]
    f32, bf16 = jnp.float32, jnp.bfloat16
    me, v, t = lax.axis_index("dp"), lax.axis_index("vocab"), lax.axis_index("tensor")
    core, my_hi = me % 2, me // 2
    other = 1 - t
    place = me * 2 + t
    mate = me + 1 - 2 * core
    core_peer, y_peer = {"dp": mate}, {"tensor": other}
    side = v % 2
    z_peer = {"vocab": v + 1 - 2 * side}
    half = CHUNKS // 2
    plane = [(place + k) % (2 * n_dp) for k in range(1, 2 * n_dp)]
    column = [(v + k) % n_v for k in range(1, n_v)]
    ring = [(me + k) % n_dp for k in range(1, n_dp)]

    barrier = pltpu.get_barrier_semaphore()
    for p in plane:
        pl.semaphore_signal(
            barrier, inc=1, device_id={"dp": p // 2, "tensor": p % 2},
            device_id_type=pl.DeviceIdType.MESH,
        )
    for z in column:
        pl.semaphore_signal(
            barrier, inc=1, device_id={"vocab": z}, device_id_type=pl.DeviceIdType.MESH
        )

    load_w = pltpu.make_async_copy(w_hbm, w, in_sem.at[0])
    load_h = pltpu.make_async_copy(h_hbm, h, in_sem.at[1])
    load_w.start()
    load_h.start()

    mask = lax.broadcasted_iota(jnp.int32, (pad, LANES), 0) == lax.broadcasted_iota(
        jnp.int32, (pad, LANES), 1
    )

    def to_row(col):
        return jnp.sum(jnp.where(mask, col, 0.0), axis=0, keepdims=True)

    def to_col(row):
        return jnp.sum(jnp.where(mask, row, 0.0), axis=1, keepdims=True)

    squares = jnp.zeros((pad, 1), f32)
    for c in range(CHUNKS):
        part = res_ref[:, c * width:(c + 1) * width].astype(f32)
        part = jnp.concatenate([part, jnp.zeros((pad - rows, width), f32)], axis=0)
        squares = squares + jnp.sum(part * part, axis=1, keepdims=True)
        x[me, c] = part.astype(bf16)
    ss[me, t] = to_row(squares)

    offset = (me * n_v + v) * vocab
    tokens = ids_ref.shape[0]

    def onehot(block):
        here = lax.broadcasted_iota(jnp.int32, (pad, tokens), 0)
        wanted = lax.broadcasted_iota(jnp.int32, (pad, tokens), 1) == here + block * rows
        ids = jnp.sum(
            jnp.where(wanted & (here < rows), ids_ref[...].reshape(1, tokens).astype(f32) + 1.0, 0.0),
            axis=1, keepdims=True,
        ).astype(jnp.int32) - 1
        return (lax.broadcasted_iota(jnp.int32, (pad, vocab), 1) == ids - offset).astype(
            f32
        ).astype(bf16)

    def mark(hi, carry):
        for k in range(2):
            he[hi, k] = onehot(hi * 2 + k)
        return carry

    pl.semaphore_wait(barrier, len(plane) + len(column))

    for p in plane:
        remote(
            ss.at[me, t], ss.at[me, t], ss_s.at[p // 2, p % 2], ss_r.at[me, t],
            {"dp": p // 2, "tensor": p % 2},
        ).start()
    for c in range(CHUNKS):
        remote(x.at[me, c], x.at[me, c], cs_s.at[my_hi, c], cs_r.at[my_hi, c], core_peer).start()
    def send_block(hi, j):
        c = side * half + j
        return remote(
            x.at[me, c], x.at[me, c], xs_s.at[hi, j], xs_r.at[my_hi, j], {"dp": hi * 2 + core}
        )

    def send_side(hi, j):
        slot = x.at[hi * 2 + core, side * half + j]
        return remote(slot, slot, zs_s.at[hi, j], zs_r.at[hi, j], z_peer)

    def send_core(hi, c):
        slot = x.at[hi * 2 + core, c]
        return remote(slot, slot, cs_s.at[hi, c], cs_r.at[hi, c], core_peer)

    for j in range(half):
        for k in range(1, n_hi):
            send_block((my_hi + k) % n_hi, j).start()

    def pass_on(hi, j):
        c = side * half + j
        slot = x.at[hi * 2 + core, c]
        remote(slot, slot, xs_s.at[hi, j], xs_r.at[hi, j], {"dp": hi * 2 + core}).wait_recv()
        send_side(hi, j).start()
        send_core(hi, c).start()

    def pass_side(hi, j):
        c = (1 - side) * half + j
        slot = x.at[hi * 2 + core, c]
        remote(slot, slot, zs_s.at[hi, j], zs_r.at[hi, j], z_peer).wait_recv()
        send_core(hi, c).start()

    def wait_core(hi):
        for c in range(CHUNKS):
            slot = x.at[hi * 2 + 1 - core, c]
            remote(slot, slot, cs_s.at[hi, c], cs_r.at[hi, c], core_peer).wait_recv()

    lax.fori_loop(0, n_hi, mark, 0)
    for p in plane:
        slot = ss.at[p // 2, p % 2]
        remote(
            slot, slot, ss_s.at[p // 2, p % 2], ss_r.at[p // 2, p % 2],
            {"dp": p // 2, "tensor": p % 2},
        ).wait_recv()

    def out_copy(hi):
        return pltpu.make_async_copy(normed.at[hi], n_out.at[hi], out_sem.at[0, hi])

    def cot_copy(hi):
        return pltpu.make_async_copy(he.at[hi, pl.ds(0, 2)], c_out.at[hi], out_sem.at[1, hi])

    def send_logits(hi):
        return remote(
            lg.at[hi, other, pl.ds(0, rows)], rl.at[hi], ls_s.at[hi], ls_r.at[hi], y_peer
        )

    def send_exp(hi):
        return remote(he.at[hi, 2 + t], he.at[hi, 2 + t], es_s.at[hi], es_r.at[hi], y_peer)

    def send_top(hi):
        return remote(ml.at[hi, t], ml.at[hi, t], ms_s.at[hi], ms_r.at[hi], y_peer)

    def pair(hi, first):
        inverse = jnp.concatenate(
            [
                to_col(lax.rsqrt((ss[hi * 2 + k, 0] + ss[hi * 2 + k, 1]) / (2 * depth) + EPSILON))
                for k in range(2)
            ],
            axis=0,
        )
        for c in range(CHUNKS):
            at = slice(c * width, (c + 1) * width)
            block = jnp.concatenate(
                [x[hi * 2, c].astype(f32), x[hi * 2 + 1, c].astype(f32)], axis=0
            )
            unit = (block * inverse).astype(bf16)
            normed[hi, :, at] = unit
            spread = unit.astype(f32)
            hid[:, at] = (spread * gain_ref[:, at]).astype(bf16)
            tan[:, at] = (spread * dir_ref[:, at]).astype(bf16)
        out_copy(hi).start()
        if first:
            load_w.wait()
        logits = jnp.dot(hid[...], w[...], preferred_element_type=f32)
        lg[hi, 0] = logits[:pad]
        lg[hi, 1] = logits[pad:]
        send_logits(hi).start()
        if first:
            load_h.wait()
        tangents = jnp.dot(hid[...], h[...], preferred_element_type=f32) + jnp.dot(
            tan[...], w[...], preferred_element_type=f32
        )
        tl[hi, 0] = tangents[:pad]
        tl[hi, 1] = tangents[pad:]

    def finish(hi):
        send_logits(hi).wait_recv()
        blank = jnp.zeros((pad - rows, vocab), f32)
        logits = jnp.concatenate([lg[hi, t][:rows] + rl[hi], blank], axis=0)
        top = jnp.max(logits, axis=1, keepdims=True)
        he[hi, 2 + t] = jnp.exp(logits - top).astype(bf16)
        ml[hi, t] = to_row(top)
        send_exp(hi).start()
        send_top(hi).start()

    def sums(hi, k):
        block = hi * 2 + k
        scaled, tangents = he[hi, 2 + k].astype(f32), tl[hi, k]
        chosen = he[hi, k].astype(f32)
        at = pl.ds(block, 1)
        st[0, at] = ml[hi, k]
        st[1, at] = to_row(jnp.sum(scaled, axis=1, keepdims=True))
        st[2, at] = to_row(jnp.sum(scaled * tangents, axis=1, keepdims=True))
        st[3, at] = to_row(jnp.sum(chosen * tangents, axis=1, keepdims=True))

    def wait_exp(hi):
        slot = he.at[hi, 2 + other]
        remote(slot, slot, es_s.at[hi], es_r.at[hi], y_peer).wait_recv()
        slot = ml.at[hi, other]
        remote(slot, slot, ms_s.at[hi], ms_r.at[hi], y_peer).wait_recv()

    def back(hi, part):
        at = slice(part * depth // 2, (part + 1) * depth // 2)
        both = jnp.concatenate([he[hi, k].astype(f32) for k in range(4)], axis=0).astype(bf16)
        turned = lax.dot_general(
            both, w[at], (((1,), (1,)), ((), ())), preferred_element_type=f32
        )
        unit = normed[hi, :, at].astype(f32)
        na[hi, :, at] = unit * turned[:2 * pad]
        nb[hi, :, at] = unit * turned[2 * pad:]

    wait_core(my_hi)
    pair(my_hi, True)

    def later(k, carry):
        hi = (my_hi + k) % n_hi
        for j in range(half):
            pass_on(hi, j)
        for j in range(half - 1):
            pass_side(hi, j)
        finish((my_hi + k - 1) % n_hi)
        pass_side(hi, half - 1)
        wait_core(hi)
        pair(hi, False)
        return carry

    def early(k, carry):
        hi = (my_hi + k) % n_hi
        sums(hi, t)
        wait_exp(hi)
        sums(hi, other)
        back(hi, 0)
        back(hi, 1)
        return carry

    lax.fori_loop(1, n_hi, later, 0)
    last = (my_hi + n_hi - 1) % n_hi
    lax.fori_loop(0, n_hi - 1, early, 0)
    finish(last)
    sums(last, t)
    wait_exp(last)
    sums(last, other)

    sz[v] = st[...]
    for z in column:
        remote(sz.at[v], sz.at[v], sz_s.at[z], sz_r.at[v], {"vocab": z}).start()
    back(last, 0)
    for z in column:
        remote(sz.at[z], sz.at[z], sz_s.at[z], sz_r.at[z], {"vocab": z}).wait_recv()
    joined = merge([[sz[z, i] for i in range(4)] for z in range(n_v)])
    for i in range(4):
        sp[me, t, i] = joined[i]
    for p in plane:
        remote(
            sp.at[me, t], sp.at[me, t], sp_s.at[p // 2, p % 2], sp_r.at[me, t],
            {"dp": p // 2, "tensor": p % 2},
        ).start()

    back(last, 1)
    for p in plane:
        slot = sp.at[p // 2, p % 2]
        remote(
            slot, slot, sp_s.at[p // 2, p % 2], sp_r.at[p // 2, p % 2],
            {"dp": p // 2, "tensor": p % 2},
        ).wait_recv()
    top, total, weighted, picked = merge(
        [[sp[d, k, i] for i in range(4)] for d in range(n_dp) for k in range(2)]
    )
    total = 0.5 * total
    sc[0] = picked - weighted / total
    sc[1] = jnp.exp(st[0] - top) / total

    def gain_part(hi, grad):
        for k in range(2):
            at, here = pl.ds(hi * 2 + k, 1), slice(k * pad, (k + 1) * pad)
            score, factor = to_col(sc[0, at]), to_col(sc[1, at])
            grad = grad + jnp.sum(
                score * (na[hi, here] - factor * nb[hi, here]), axis=0, keepdims=True
            )
        return grad

    gz[v] = lax.fori_loop(0, n_hi, gain_part, jnp.zeros((1, depth), f32))
    for z in column:
        remote(gz.at[v], gz.at[v], gz_s.at[z], gz_r.at[v], {"vocab": z}).start()

    def cotangents(hi, carry):
        for k in range(2):
            at = pl.ds(hi * 2 + k, 1)
            score, factor = to_col(sc[0, at]), to_col(sc[1, at])
            chosen = he[hi, k].astype(f32)
            he[hi, k] = (score * (chosen - he[hi, 2 + k].astype(f32) * factor)).astype(bf16)
        cot_copy(hi).start()
        return carry

    lax.fori_loop(0, n_hi, cotangents, 0)
    for z in column:
        remote(gz.at[z], gz.at[z], gz_s.at[z], gz_r.at[z], {"vocab": z}).wait_recv()
    gp[me] = sum(gz[z] for z in range(n_v))
    for d in ring:
        remote(gp.at[me], gp.at[me], gp_s.at[d], gp_r.at[me], {"dp": d}).start()
    for d in ring:
        remote(gp.at[d], gp.at[d], gp_s.at[d], gp_r.at[d], {"dp": d}).wait_recv()
    g_out[...] = sum(gp[d] for d in range(n_dp))

    for p in plane:
        device = {"dp": p // 2, "tensor": p % 2}
        mine = ss.at[me, t]
        remote(mine, mine, ss_s.at[p // 2, p % 2], ss_r.at[me, t], device).wait_send()
        mine = sp.at[me, t]
        remote(mine, mine, sp_s.at[p // 2, p % 2], sp_r.at[me, t], device).wait_send()
    for z in column:
        remote(sz.at[v], sz.at[v], sz_s.at[z], sz_r.at[v], {"vocab": z}).wait_send()
        remote(gz.at[v], gz.at[v], gz_s.at[z], gz_r.at[v], {"vocab": z}).wait_send()
    for d in ring:
        remote(gp.at[me], gp.at[me], gp_s.at[d], gp_r.at[me], {"dp": d}).wait_send()
    for k in range(n_hi):
        hi = (my_hi + k) % n_hi
        for c in range(CHUNKS):
            send_core(hi, c).wait_send()
        if k:
            for j in range(half):
                send_block(hi, j).wait_send()
                send_side(hi, j).wait_send()
        send_logits(hi).wait_send()
        send_exp(hi).wait_send()
        send_top(hi).wait_send()
        out_copy(hi).wait()
        cot_copy(hi).wait()


def local(n_dp, n_v, residual, norm_gain, gain_dir, head_weight, head_dir, sampled):
    n_hi = n_dp // 2
    rows, depth = residual.shape
    vocab = head_weight.shape[1]
    pad = -(-rows // 16) * 16
    f32, bf16 = jnp.float32, jnp.bfloat16
    vmem = pl.BlockSpec(memory_space=pltpu.VMEM)
    hbm = pl.BlockSpec(memory_space=pl.ANY)
    dma = pltpu.SemaphoreType.DMA
    pairs = [
        dma((n_dp, 2)), dma((n_dp, 2)),
        dma((n_hi, CHUNKS)), dma((n_hi, CHUNKS)), dma((n_hi, CHUNKS)), dma((n_hi, CHUNKS)),
        dma((n_hi, CHUNKS)), dma((n_hi, CHUNKS)),
        dma((n_hi,)), dma((n_hi,)), dma((n_hi,)), dma((n_hi,)), dma((n_hi,)), dma((n_hi,)),
        dma((n_v,)), dma((n_v,)), dma((n_dp, 2)), dma((n_dp, 2)),
        dma((n_v,)), dma((n_v,)), dma((n_dp,)), dma((n_dp,)),
    ]
    normed, cotangent, gain = pl.pallas_call(
        functools.partial(kernel, n_dp, n_v),
        out_shape=(
            jax.ShapeDtypeStruct((n_hi, 2 * pad, depth), bf16),
            jax.ShapeDtypeStruct((n_hi, 2, pad, vocab), bf16),
            jax.ShapeDtypeStruct((1, depth), f32),
        ),
        in_specs=[vmem, vmem, vmem, vmem] + [hbm, hbm],
        out_specs=(hbm, hbm, vmem),
        scratch_shapes=[
            pltpu.VMEM((n_dp, CHUNKS, pad, depth // CHUNKS), bf16),
            pltpu.VMEM((depth, vocab), bf16),
            pltpu.VMEM((depth, vocab), bf16),
            pltpu.VMEM((n_hi, 2 * pad, depth), bf16),
            pltpu.VMEM((2 * pad, depth), bf16),
            pltpu.VMEM((2 * pad, depth), bf16),
            pltpu.VMEM((n_hi, 2, pad, vocab), f32),
            pltpu.VMEM((n_hi, 2, pad, vocab), f32),
            pltpu.VMEM((n_hi, rows, vocab), f32),
            pltpu.VMEM((n_hi, 4, pad, vocab), bf16),
            pltpu.VMEM((n_hi, 2 * pad, depth), f32),
            pltpu.VMEM((n_hi, 2 * pad, depth), f32),
            pltpu.VMEM((n_dp, 2, 1, LANES), f32),
            pltpu.VMEM((n_hi, 2, 1, LANES), f32),
            pltpu.VMEM((4, n_dp, LANES), f32),
            pltpu.VMEM((n_v, 4, n_dp, LANES), f32),
            pltpu.VMEM((n_dp, 2, 4, n_dp, LANES), f32),
            pltpu.VMEM((2, n_dp, LANES), f32),
            pltpu.VMEM((n_v, 1, depth), f32),
            pltpu.VMEM((n_dp, 1, depth), f32),
            dma((2,)), dma((2, n_hi)),
        ] + pairs,
        compiler_params=pltpu.CompilerParams(
            collective_id=0, has_side_effects=True, vmem_limit_bytes=62 * MIB
        ),
        cost_estimate=pl.CostEstimate(
            flops=10 * n_dp * rows * depth * vocab,
            bytes_accessed=4 * depth * vocab,
            transcendentals=n_dp * rows * vocab,
        ),
    )(residual, norm_gain.reshape(1, depth), gain_dir.reshape(1, depth), sampled, head_weight, head_dir)
    product = lax.dot_general(
        normed.reshape(n_dp * pad, depth), cotangent.reshape(n_dp * pad, vocab),
        (((0,), (0,)), ((), ())), preferred_element_type=f32,
    )
    return norm_gain[:, None] * product, gain.reshape(depth)


def solution(mesh):
    assert mesh.shape["tensor"] == 2 and mesh.shape["dp"] % 2 == 0
    in_specs = (
        P("dp", "tensor"),
        P("tensor"),
        P("tensor"),
        P("tensor", ("dp", "vocab")),
        P("tensor", ("dp", "vocab")),
        P(),
    )
    out_specs = (P("tensor", ("dp", "vocab")), P("tensor"))
    return jax.shard_map(
        functools.partial(local, mesh.shape["dp"], mesh.shape["vocab"]),
        mesh=mesh, in_specs=in_specs, out_specs=out_specs, check_vma=False,
    )
```

```python
import functools

import jax
import jax.numpy as jnp
from jax import lax
from jax.experimental import pallas as pl
from jax.experimental.pallas import tpu as pltpu
from jax.sharding import PartitionSpec as P

EPSILON = 1e-06
LANES = 128
CHUNKS = 4
MIB = 1024 * 1024


def remote(src, dst, send_sem, recv_sem, device):
    return pltpu.make_async_remote_copy(
        src_ref=src,
        dst_ref=dst,
        send_sem=send_sem,
        recv_sem=recv_sem,
        device_id=device,
        device_id_type=pl.DeviceIdType.MESH,
    )


def merge(parts):
    top = functools.reduce(jnp.maximum, [part[0] for part in parts])
    scales = [jnp.exp(part[0] - top) for part in parts]
    total = sum(part[1] * scale for part, scale in zip(parts, scales))
    weighted = sum(part[2] * scale for part, scale in zip(parts, scales))
    picked = sum(part[3] for part in parts)
    return top, total, weighted, picked


def kernel(
    n_dp, n_v, res_ref, gain_ref, dir_ref, ids_ref, w_hbm, h_hbm, n_out, c_out, g_out,
    x, w, h, normed, hid, tan, lg, tl, rl, he, na, nb, ss, ml, st, sz, sp, sc,
    gz, gp,
    in_sem, out_sem, ss_s, ss_r, xs_s, xs_r, zs_s, zs_r, cs_s, cs_r, ls_s, ls_r, es_s, es_r, ms_s, ms_r,
    sz_s, sz_r, sp_s, sp_r, gz_s, gz_r, gp_s, gp_r,
):
    n_hi = n_dp // 2
    rows, depth = res_ref.shape
    vocab = w.shape[1]
    pad = x.shape[2]
    width = x.shape[3]
    f32, bf16 = jnp.float32, jnp.bfloat16
    me, v, t = lax.axis_index("dp"), lax.axis_index("vocab"), lax.axis_index("tensor")
    core, my_hi = me % 2, me // 2
    other = 1 - t
    place = me * 2 + t
    mate = me + 1 - 2 * core
    core_peer, y_peer = {"dp": mate}, {"tensor": other}
    side = v % 2
    z_peer = {"vocab": v + 1 - 2 * side}
    half = CHUNKS // 2
    plane = [(place + k) % (2 * n_dp) for k in range(1, 2 * n_dp)]
    column = [(v + k) % n_v for k in range(1, n_v)]
    ring = [(me + k) % n_dp for k in range(1, n_dp)]

    barrier = pltpu.get_barrier_semaphore()
    for p in plane:
        pl.semaphore_signal(
            barrier, inc=1, device_id={"dp": p // 2, "tensor": p % 2},
            device_id_type=pl.DeviceIdType.MESH,
        )
    for z in column:
        pl.semaphore_signal(
            barrier, inc=1, device_id={"vocab": z}, device_id_type=pl.DeviceIdType.MESH
        )

    load_w = pltpu.make_async_copy(w_hbm, w, in_sem.at[0])
    load_h = pltpu.make_async_copy(h_hbm, h, in_sem.at[1])
    load_w.start()
    load_h.start()

    mask = lax.broadcasted_iota(jnp.int32, (pad, LANES), 0) == lax.broadcasted_iota(
        jnp.int32, (pad, LANES), 1
    )

    def to_row(col):
        return jnp.sum(jnp.where(mask, col, 0.0), axis=0, keepdims=True)

    def to_col(row):
        return jnp.sum(jnp.where(mask, row, 0.0), axis=1, keepdims=True)

    squares = jnp.zeros((pad, 1), f32)
    for c in range(CHUNKS):
        part = res_ref[:, c * width:(c + 1) * width].astype(f32)
        part = jnp.concatenate([part, jnp.zeros((pad - rows, width), f32)], axis=0)
        squares = squares + jnp.sum(part * part, axis=1, keepdims=True)
        x[me, c] = part.astype(bf16)
    ss[me, t] = to_row(squares)

    offset = (me * n_v + v) * vocab
    tokens = ids_ref.shape[0]

    def onehot(block):
        here = lax.broadcasted_iota(jnp.int32, (pad, tokens), 0)
        wanted = lax.broadcasted_iota(jnp.int32, (pad, tokens), 1) == here + block * rows
        ids = jnp.sum(
            jnp.where(wanted & (here < rows), ids_ref[...].reshape(1, tokens).astype(f32) + 1.0, 0.0),
            axis=1, keepdims=True,
        ).astype(jnp.int32) - 1
        return (lax.broadcasted_iota(jnp.int32, (pad, vocab), 1) == ids - offset).astype(
            f32
        ).astype(bf16)

    def mark(hi, carry):
        for k in range(2):
            he[hi, k] = onehot(hi * 2 + k)
        return carry

    pl.semaphore_wait(barrier, len(plane) + len(column))

    for p in plane:
        remote(
            ss.at[me, t], ss.at[me, t], ss_s.at[p // 2, p % 2], ss_r.at[me, t],
            {"dp": p // 2, "tensor": p % 2},
        ).start()
    for c in range(CHUNKS):
        remote(x.at[me, c], x.at[me, c], cs_s.at[my_hi, c], cs_r.at[my_hi, c], core_peer).start()
    def send_block(hi, j):
        c = side * half + j
        return remote(
            x.at[me, c], x.at[me, c], xs_s.at[hi, j], xs_r.at[my_hi, j], {"dp": hi * 2 + core}
        )

    def send_side(hi, j):
        slot = x.at[hi * 2 + core, side * half + j]
        return remote(slot, slot, zs_s.at[hi, j], zs_r.at[hi, j], z_peer)

    def send_core(hi, c):
        slot = x.at[hi * 2 + core, c]
        return remote(slot, slot, cs_s.at[hi, c], cs_r.at[hi, c], core_peer)

    for j in range(half):
        for k in range(1, n_hi):
            send_block((my_hi + k) % n_hi, j).start()

    def pass_on(hi, j):
        c = side * half + j
        slot = x.at[hi * 2 + core, c]
        remote(slot, slot, xs_s.at[hi, j], xs_r.at[hi, j], {"dp": hi * 2 + core}).wait_recv()
        send_side(hi, j).start()
        send_core(hi, c).start()

    def pass_side(hi, j):
        c = (1 - side) * half + j
        slot = x.at[hi * 2 + core, c]
        remote(slot, slot, zs_s.at[hi, j], zs_r.at[hi, j], z_peer).wait_recv()
        send_core(hi, c).start()

    def wait_core(hi):
        for c in range(CHUNKS):
            slot = x.at[hi * 2 + 1 - core, c]
            remote(slot, slot, cs_s.at[hi, c], cs_r.at[hi, c], core_peer).wait_recv()

    lax.fori_loop(0, n_hi, mark, 0)
    for p in plane:
        slot = ss.at[p // 2, p % 2]
        remote(
            slot, slot, ss_s.at[p // 2, p % 2], ss_r.at[p // 2, p % 2],
            {"dp": p // 2, "tensor": p % 2},
        ).wait_recv()

    def out_copy(hi):
        return pltpu.make_async_copy(normed.at[hi], n_out.at[hi], out_sem.at[0, hi])

    def cot_copy(hi):
        return pltpu.make_async_copy(he.at[hi, pl.ds(0, 2)], c_out.at[hi], out_sem.at[1, hi])

    def send_logits(hi):
        return remote(
            lg.at[hi, other, pl.ds(0, rows)], rl.at[hi], ls_s.at[hi], ls_r.at[hi], y_peer
        )

    def send_exp(hi):
        return remote(he.at[hi, 2 + t], he.at[hi, 2 + t], es_s.at[hi], es_r.at[hi], y_peer)

    def send_top(hi):
        return remote(ml.at[hi, t], ml.at[hi, t], ms_s.at[hi], ms_r.at[hi], y_peer)

    def pair(hi, first):
        inverse = jnp.concatenate(
            [
                to_col(lax.rsqrt((ss[hi * 2 + k, 0] + ss[hi * 2 + k, 1]) / (2 * depth) + EPSILON))
                for k in range(2)
            ],
            axis=0,
        )
        for c in range(CHUNKS):
            at = slice(c * width, (c + 1) * width)
            block = jnp.concatenate(
                [x[hi * 2, c].astype(f32), x[hi * 2 + 1, c].astype(f32)], axis=0
            )
            unit = (block * inverse).astype(bf16)
            normed[hi, :, at] = unit
            spread = unit.astype(f32)
            hid[:, at] = (spread * gain_ref[:, at]).astype(bf16)
            tan[:, at] = (spread * dir_ref[:, at]).astype(bf16)
        out_copy(hi).start()
        if first:
            load_w.wait()
        logits = jnp.dot(hid[...], w[...], preferred_element_type=f32)
        lg[hi, 0] = logits[:pad]
        lg[hi, 1] = logits[pad:]
        send_logits(hi).start()
        if first:
            load_h.wait()
        tangents = jnp.dot(hid[...], h[...], preferred_element_type=f32) + jnp.dot(
            tan[...], w[...], preferred_element_type=f32
        )
        tl[hi, 0] = tangents[:pad]
        tl[hi, 1] = tangents[pad:]

    def finish(hi):
        send_logits(hi).wait_recv()
        blank = jnp.zeros((pad - rows, vocab), f32)
        logits = jnp.concatenate([lg[hi, t][:rows] + rl[hi], blank], axis=0)
        top = jnp.max(logits, axis=1, keepdims=True)
        he[hi, 2 + t] = jnp.exp(logits - top).astype(bf16)
        ml[hi, t] = to_row(top)
        send_exp(hi).start()
        send_top(hi).start()

    def sums(hi, k):
        block = hi * 2 + k
        scaled, tangents = he[hi, 2 + k].astype(f32), tl[hi, k]
        chosen = he[hi, k].astype(f32)
        at = pl.ds(block, 1)
        st[0, at] = ml[hi, k]
        st[1, at] = to_row(jnp.sum(scaled, axis=1, keepdims=True))
        st[2, at] = to_row(jnp.sum(scaled * tangents, axis=1, keepdims=True))
        st[3, at] = to_row(jnp.sum(chosen * tangents, axis=1, keepdims=True))

    def wait_exp(hi):
        slot = he.at[hi, 2 + other]
        remote(slot, slot, es_s.at[hi], es_r.at[hi], y_peer).wait_recv()
        slot = ml.at[hi, other]
        remote(slot, slot, ms_s.at[hi], ms_r.at[hi], y_peer).wait_recv()

    def back(hi, part):
        at = slice(part * depth // 2, (part + 1) * depth // 2)
        both = jnp.concatenate([he[hi, k].astype(f32) for k in range(4)], axis=0).astype(bf16)
        turned = lax.dot_general(
            both, w[at], (((1,), (1,)), ((), ())), preferred_element_type=f32
        )
        unit = normed[hi, :, at].astype(f32)
        na[hi, :, at] = unit * turned[:2 * pad]
        nb[hi, :, at] = unit * turned[2 * pad:]

    wait_core(my_hi)
    pair(my_hi, True)

    def later(k, carry):
        hi = (my_hi + k) % n_hi
        for j in range(half):
            pass_on(hi, j)
        for j in range(half - 1):
            pass_side(hi, j)
        finish((my_hi + k - 1) % n_hi)
        pass_side(hi, half - 1)
        wait_core(hi)
        pair(hi, False)
        return carry

    def early(k, carry):
        hi = (my_hi + k) % n_hi
        sums(hi, t)
        wait_exp(hi)
        sums(hi, other)
        return carry

    def early_back(k, carry):
        hi = (my_hi + k) % n_hi
        back(hi, 0)
        back(hi, 1)
        return carry

    lax.fori_loop(1, n_hi, later, 0)
    last = (my_hi + n_hi - 1) % n_hi
    lax.fori_loop(0, n_hi - 1, early, 0)
    finish(last)
    sums(last, t)
    lax.fori_loop(0, n_hi - 1, early_back, 0)
    wait_exp(last)
    sums(last, other)

    sz[v] = st[...]
    for z in column:
        remote(sz.at[v], sz.at[v], sz_s.at[z], sz_r.at[v], {"vocab": z}).start()
    back(last, 0)
    for z in column:
        remote(sz.at[z], sz.at[z], sz_s.at[z], sz_r.at[z], {"vocab": z}).wait_recv()
    joined = merge([[sz[z, i] for i in range(4)] for z in range(n_v)])
    for i in range(4):
        sp[me, t, i] = joined[i]
    for p in plane:
        remote(
            sp.at[me, t], sp.at[me, t], sp_s.at[p // 2, p % 2], sp_r.at[me, t],
            {"dp": p // 2, "tensor": p % 2},
        ).start()

    back(last, 1)
    for p in plane:
        slot = sp.at[p // 2, p % 2]
        remote(
            slot, slot, sp_s.at[p // 2, p % 2], sp_r.at[p // 2, p % 2],
            {"dp": p // 2, "tensor": p % 2},
        ).wait_recv()
    top, total, weighted, picked = merge(
        [[sp[d, k, i] for i in range(4)] for d in range(n_dp) for k in range(2)]
    )
    total = 0.5 * total
    sc[0] = picked - weighted / total
    sc[1] = jnp.exp(st[0] - top) / total

    def gain_part(hi, grad):
        for k in range(2):
            at, here = pl.ds(hi * 2 + k, 1), slice(k * pad, (k + 1) * pad)
            score, factor = to_col(sc[0, at]), to_col(sc[1, at])
            grad = grad + jnp.sum(
                score * (na[hi, here] - factor * nb[hi, here]), axis=0, keepdims=True
            )
        return grad

    gz[v] = lax.fori_loop(0, n_hi, gain_part, jnp.zeros((1, depth), f32))
    for z in column:
        remote(gz.at[v], gz.at[v], gz_s.at[z], gz_r.at[v], {"vocab": z}).start()

    def cotangents(hi, carry):
        for k in range(2):
            at = pl.ds(hi * 2 + k, 1)
            score, factor = to_col(sc[0, at]), to_col(sc[1, at])
            chosen = he[hi, k].astype(f32)
            he[hi, k] = (score * (chosen - he[hi, 2 + k].astype(f32) * factor)).astype(bf16)
        cot_copy(hi).start()
        return carry

    lax.fori_loop(0, n_hi, cotangents, 0)
    for z in column:
        remote(gz.at[z], gz.at[z], gz_s.at[z], gz_r.at[z], {"vocab": z}).wait_recv()
    gp[me] = sum(gz[z] for z in range(n_v))
    for d in ring:
        remote(gp.at[me], gp.at[me], gp_s.at[d], gp_r.at[me], {"dp": d}).start()
    for d in ring:
        remote(gp.at[d], gp.at[d], gp_s.at[d], gp_r.at[d], {"dp": d}).wait_recv()
    g_out[...] = sum(gp[d] for d in range(n_dp))

    for p in plane:
        device = {"dp": p // 2, "tensor": p % 2}
        mine = ss.at[me, t]
        remote(mine, mine, ss_s.at[p // 2, p % 2], ss_r.at[me, t], device).wait_send()
        mine = sp.at[me, t]
        remote(mine, mine, sp_s.at[p // 2, p % 2], sp_r.at[me, t], device).wait_send()
    for z in column:
        remote(sz.at[v], sz.at[v], sz_s.at[z], sz_r.at[v], {"vocab": z}).wait_send()
        remote(gz.at[v], gz.at[v], gz_s.at[z], gz_r.at[v], {"vocab": z}).wait_send()
    for d in ring:
        remote(gp.at[me], gp.at[me], gp_s.at[d], gp_r.at[me], {"dp": d}).wait_send()
    for k in range(n_hi):
        hi = (my_hi + k) % n_hi
        for c in range(CHUNKS):
            send_core(hi, c).wait_send()
        if k:
            for j in range(half):
                send_block(hi, j).wait_send()
                send_side(hi, j).wait_send()
        send_logits(hi).wait_send()
        send_exp(hi).wait_send()
        send_top(hi).wait_send()
        out_copy(hi).wait()
        cot_copy(hi).wait()


def local(n_dp, n_v, residual, norm_gain, gain_dir, head_weight, head_dir, sampled):
    n_hi = n_dp // 2
    rows, depth = residual.shape
    vocab = head_weight.shape[1]
    pad = -(-rows // 16) * 16
    f32, bf16 = jnp.float32, jnp.bfloat16
    vmem = pl.BlockSpec(memory_space=pltpu.VMEM)
    hbm = pl.BlockSpec(memory_space=pl.ANY)
    dma = pltpu.SemaphoreType.DMA
    pairs = [
        dma((n_dp, 2)), dma((n_dp, 2)),
        dma((n_hi, CHUNKS)), dma((n_hi, CHUNKS)), dma((n_hi, CHUNKS)), dma((n_hi, CHUNKS)),
        dma((n_hi, CHUNKS)), dma((n_hi, CHUNKS)),
        dma((n_hi,)), dma((n_hi,)), dma((n_hi,)), dma((n_hi,)), dma((n_hi,)), dma((n_hi,)),
        dma((n_v,)), dma((n_v,)), dma((n_dp, 2)), dma((n_dp, 2)),
        dma((n_v,)), dma((n_v,)), dma((n_dp,)), dma((n_dp,)),
    ]
    normed, cotangent, gain = pl.pallas_call(
        functools.partial(kernel, n_dp, n_v),
        out_shape=(
            jax.ShapeDtypeStruct((n_hi, 2 * pad, depth), bf16),
            jax.ShapeDtypeStruct((n_hi, 2, pad, vocab), bf16),
            jax.ShapeDtypeStruct((1, depth), f32),
        ),
        in_specs=[vmem, vmem, vmem, vmem] + [hbm, hbm],
        out_specs=(hbm, hbm, vmem),
        scratch_shapes=[
            pltpu.VMEM((n_dp, CHUNKS, pad, depth // CHUNKS), bf16),
            pltpu.VMEM((depth, vocab), bf16),
            pltpu.VMEM((depth, vocab), bf16),
            pltpu.VMEM((n_hi, 2 * pad, depth), bf16),
            pltpu.VMEM((2 * pad, depth), bf16),
            pltpu.VMEM((2 * pad, depth), bf16),
            pltpu.VMEM((n_hi, 2, pad, vocab), f32),
            pltpu.VMEM((n_hi, 2, pad, vocab), f32),
            pltpu.VMEM((n_hi, rows, vocab), f32),
            pltpu.VMEM((n_hi, 4, pad, vocab), bf16),
            pltpu.VMEM((n_hi, 2 * pad, depth), f32),
            pltpu.VMEM((n_hi, 2 * pad, depth), f32),
            pltpu.VMEM((n_dp, 2, 1, LANES), f32),
            pltpu.VMEM((n_hi, 2, 1, LANES), f32),
            pltpu.VMEM((4, n_dp, LANES), f32),
            pltpu.VMEM((n_v, 4, n_dp, LANES), f32),
            pltpu.VMEM((n_dp, 2, 4, n_dp, LANES), f32),
            pltpu.VMEM((2, n_dp, LANES), f32),
            pltpu.VMEM((n_v, 1, depth), f32),
            pltpu.VMEM((n_dp, 1, depth), f32),
            dma((2,)), dma((2, n_hi)),
        ] + pairs,
        compiler_params=pltpu.CompilerParams(
            collective_id=0, has_side_effects=True, vmem_limit_bytes=62 * MIB
        ),
        cost_estimate=pl.CostEstimate(
            flops=10 * n_dp * rows * depth * vocab,
            bytes_accessed=4 * depth * vocab,
            transcendentals=n_dp * rows * vocab,
        ),
    )(residual, norm_gain.reshape(1, depth), gain_dir.reshape(1, depth), sampled, head_weight, head_dir)
    product = lax.dot_general(
        normed.reshape(n_dp * pad, depth), cotangent.reshape(n_dp * pad, vocab),
        (((0,), (0,)), ((), ())), preferred_element_type=f32,
    )
    return norm_gain[:, None] * product, gain.reshape(depth)


def solution(mesh):
    assert mesh.shape["tensor"] == 2 and mesh.shape["dp"] % 2 == 0
    in_specs = (
        P("dp", "tensor"),
        P("tensor"),
        P("tensor"),
        P("tensor", ("dp", "vocab")),
        P("tensor", ("dp", "vocab")),
        P(),
    )
    out_specs = (P("tensor", ("dp", "vocab")), P("tensor"))
    return jax.shard_map(
        functools.partial(local, mesh.shape["dp"], mesh.shape["vocab"]),
        mesh=mesh, in_specs=in_specs, out_specs=out_specs, check_vma=False,
    )
```
